256 devices in a mesh: region: 64 (over x, z, core), obs: 4 (over y).
Axes of the slice: x: 4, y: 4, z: 8, core: 2. Of those that a mesh axis runs over, the one named last changes fastest.
Arguments:
- state_pert: bfloat16 [8192, 128, 512], P('region', None, 'obs'), may hold values from -6 to 6
- state_mean: float32 [8192, 512], P('region', 'obs'), may hold values from -6 to 6
- obs_pert: bfloat16 [8192, 128, 128], P(('region', 'obs')), may hold values from -6 to 6
- innov: float32 [8192, 128], P(('region', 'obs')), may hold values from -6 to 6
- obs_weight: float32 [8192, 128], P(('region', 'obs')), may hold values from 0.1 to 1
- block_type: int32 [8192], P(('region', 'obs')), may hold values from 0 to 7, as said below
- type_prec: float32 [8], replicated, may hold values from 0.3 to 3
- block_list: int32 [8192, 8], P('region', 'obs'), may hold values from 0 to 31
- block_count: int32 [8192, 4], P('region', 'obs'), may hold values from 1 to 2
- obs_clusters: int32 [64], replicated, may hold values from 1 to 128, 2048 in all
Outputs:
- analysis: bfloat16 [8192, 128, 512], P('region', None, 'obs')
The draws below stay inside these ranges and needn't reach their ends.
Inputs may be any that keep to these rules, and one draw needn't show every extreme that they name: `block_type`: blocks held on index o of obs have types o * 2 to (o + 1) * 2 - 1. `block_list`: entries name blocks of the pool of the cluster's own tile and the entry's index of obs. `obs_clusters`: the counts sum to 2048.
All inputs are finite; a program needn't handle non-finite values.
Results may differ from the reference program's by a relative error of at most 0.0021.
Values may be sent and summed in bfloat16 or wider, within the bound.
A program may use at most 128 MiB of HBM per device.

```python
import math
import jax
import jax.numpy as jnp
import numpy as np
from jax import lax

K = 128
OB = 128
CL_DEV = 128
POOL = 32
MAXB = 2
TYPE_DEV = 2
ITERS = 12
POINTS = 512
NCL = 8192
NBLK = 8192
NTYPES = 8
OBSERVED = 2048
N_REGION = 64
N_OBS = 4


def draw_block_type(key, part):
    key = jax.random.fold_in(key, 7)
    position = jnp.arange(NBLK, dtype=jnp.int32)
    shard = position // POOL % N_OBS
    within = jax.random.randint(key, (NBLK,), 0, TYPE_DEV, dtype=jnp.int32)
    return (shard * TYPE_DEV + within).astype(jnp.int32)


def with_ends(values, own_key, least, high):
    dims = values.shape
    index_at = [jax.random.randint(jax.random.fold_in(own_key, axis), (), 0, dims[axis]) for axis in range(len(dims))]
    values = values.at[tuple(index_at)].set(least)
    longest = dims.index(max(dims))
    index_at[longest] = (index_at[longest] + 1) % dims[longest]
    return values.at[tuple(index_at)].set(high)


def block_scale(stream_key, shape, pieces, least, largest):
    factor_of = 1.0
    for dim, parts in pieces:
        draws = jax.random.uniform(jax.random.fold_in(jax.random.fold_in(stream_key, 6), dim), (parts,), jnp.float32, least / len(pieces), largest / len(pieces))
        factor_of = factor_of * jnp.repeat(jnp.exp(draws), shape[dim] // parts).reshape((-1,) + (1,) * (len(shape) - 1 - dim))
    return factor_of


def split_up(amount, total, most, slope):
    portions = [(1 << 20) // math.isqrt(grade ** slope) + 1 for grade in range(2, amount + 1)]
    rest, given = total - most - (amount - 1), [1] * (amount - 1)
    while rest > 0:
        movable = [i for i in range(amount - 1) if given[i] < most]
        whole, remaining = sum([portions[i] for i in movable]), rest
        for i in movable:
            more = min(most - given[i], max(1, remaining * portions[i] // whole), rest)
            given[i] = given[i] + more
            rest = rest - more
    return np.array([most] + given)


def uneven_parts(rng, number_of, total, limit, lean):
    if number_of == 2:
        one = jax.random.randint(rng, (), max(1, total - limit), min(limit, total - 1) + 1)
        return jnp.stack([one, total - one])
    sizes = jnp.asarray(split_up(number_of, total, limit, lean), jnp.int32)
    pairs = (number_of - 1) // 2
    giver, sink = sizes[1:1 + 2 * pairs:2], sizes[2:2 + 2 * pairs:2]
    margin = jnp.minimum(giver - 1, limit - sink)
    moved = jax.random.randint(jax.random.fold_in(rng, 1), (pairs,), 0, 1 << 20) % (margin + 1)
    sizes = sizes.at[1:1 + 2 * pairs:2].set(giver - moved).at[2:2 + 2 * pairs:2].set(sink + moved)
    return sizes[jax.random.permutation(jax.random.fold_in(rng, 2), number_of)]


def bell_draw(own_key, extent, spread, reach, split=(), kind=jnp.bfloat16):
    level = block_scale(own_key, extent, split, -0.22, 0.18) if split else 1.0
    drawn = jax.random.normal(own_key, extent, jnp.float32) * spread * level
    return jnp.minimum(jnp.maximum(drawn, -reach), reach).astype(kind)


def setup_inputs(seed: int = 0) -> dict:
    key_of = jax.random.split(jax.random.key(seed), 11)
    state_pert = bell_draw(key_of[0], (NCL, K, POINTS), 1.0, 6.0, ((0, 64), (2, 4)))
    state_mean = bell_draw(key_of[1], (NCL, POINTS), 1.0, 6.0, ((0, 64), (1, 4)), jnp.float32)
    obs_pert = bell_draw(key_of[2], (NBLK, K, OB), 1.0, 6.0, ((0, 256),))
    innov = bell_draw(key_of[3], (NBLK, OB), 1.0, 6.0, ((0, 256),), jnp.float32)
    obs_weight = jnp.clip(0.1 + 0.9 * jax.random.uniform(key_of[4], (NBLK, OB), jnp.float32) ** block_scale(key_of[4], (NBLK, OB), ((0, 256),), -0.2, 0.2), 0.1, 1.0)
    block_type = draw_block_type(jax.random.fold_in(key_of[10], 71), 0)
    type_prec = jnp.clip(jnp.exp(jax.random.uniform(key_of[6], (NTYPES,), jnp.float32, math.log(0.3), math.log(3.0))), 0.3, 3.0)
    block_list = with_ends(jax.random.randint(key_of[7], (NCL, N_OBS * MAXB), 0, POOL), jax.random.fold_in(key_of[7], 1), 0, POOL - 1).astype(jnp.int32)
    block_count = with_ends(jax.random.randint(key_of[8], (NCL, N_OBS), 1, MAXB + 1), jax.random.fold_in(key_of[8], 1), 1, MAXB).astype(jnp.int32)
    obs_clusters = uneven_parts(key_of[9], N_REGION, OBSERVED, CL_DEV, 2).astype(jnp.int32)
    return dict(state_pert=state_pert, state_mean=state_mean, obs_pert=obs_pert, innov=innov, obs_weight=obs_weight, block_type=block_type, type_prec=type_prec, block_list=block_list, block_count=block_count, obs_clusters=obs_clusters)


def product(left, right):
    return jnp.einsum('cij,cjk->cik', left, right, precision=lax.Precision.HIGHEST)

def transform(gram_sums, projected, members):
    identity = jnp.eye(members, dtype=jnp.float32)
    matrix = identity + gram_sums / (members - 1.0)
    norm_sum = jnp.sqrt(lax.optimization_barrier(jnp.sum(matrix * matrix, axis=(1, 2))))
    iterate_y = matrix / norm_sum[:, None, None]
    iterate_z = jnp.broadcast_to(identity, matrix.shape)

    def newton_step(turn, state_pair):
        current_y, current_z = state_pair
        turn_matrix = 1.5 * identity - 0.5 * product(current_z, current_y)
        return (product(current_y, turn_matrix), product(turn_matrix, current_z))
    iterate_y, iterate_z = lax.fori_loop(0, ITERS, newton_step, (iterate_y, iterate_z))
    inverse = product(iterate_z, iterate_z) / norm_sum[:, None, None]
    mean_weights = jnp.einsum('ckl,cl->ck', inverse, projected, precision=lax.Precision.HIGHEST) / (members - 1.0)
    sqrt_inverse = iterate_z / jnp.sqrt(norm_sum)[:, None, None]
    return (sqrt_inverse + mean_weights[:, :, None]).astype(jnp.bfloat16)

def by_tile(array):
    return array.reshape((N_REGION, CL_DEV) + array.shape[1:])

def reference(state_pert, state_mean, obs_pert, innov, obs_weight, block_type, type_prec, block_list, block_count, obs_clusters):
    members = obs_pert.shape[1]
    precision_row = type_prec[block_type]
    weighted = obs_weight * precision_row[:, None]
    weight_rows = weighted.astype(jnp.bfloat16)
    weighted_innov = (weighted * innov).astype(jnp.bfloat16)
    entries = N_OBS * MAXB
    entry_shard = jnp.arange(entries, dtype=jnp.int32) // MAXB
    entry_slot = jnp.arange(entries, dtype=jnp.int32) % MAXB
    cluster_ids = jnp.arange(NCL, dtype=jnp.int32)
    tile_index = cluster_ids // CL_DEV
    block_ids = ((tile_index[:, None] * N_OBS + entry_shard[None, :]) * POOL + block_list).astype(jnp.int32)
    live_mask = entry_slot[None, :] < block_count[:, entry_shard]
    observed = cluster_ids % CL_DEV < obs_clusters[tile_index]

    def tile_analysis(inputs):
        block_group, mask_group, seen_group, pert_group, mean_group = inputs
        cluster_pert = obs_pert[block_group].astype(jnp.float32)
        zero_value = jnp.zeros((), jnp.bfloat16)
        cluster_weights = jnp.where(mask_group[:, :, None], weight_rows[block_group], zero_value).astype(jnp.float32)
        cluster_innov = jnp.where(mask_group[:, :, None], weighted_innov[block_group], zero_value).astype(jnp.float32)
        scaled = (cluster_pert * cluster_weights[:, :, None, :]).astype(jnp.bfloat16)
        scaled = lax.optimization_barrier(scaled).astype(jnp.float32)
        gram_sums = jnp.einsum('cbko,cblo->ckl', cluster_pert, scaled, precision=lax.Precision.HIGHEST)
        projected = jnp.einsum('cbko,cbo->ck', cluster_pert, cluster_innov, precision=lax.Precision.HIGHEST)
        solved = transform(gram_sums, projected, members)
        identity = jnp.eye(members, dtype=jnp.bfloat16)
        transform_rows = jnp.where(seen_group[:, None, None], solved, identity[None]).astype(jnp.float32)
        mixed = jnp.einsum('cij,cip->cjp', transform_rows, pert_group.astype(jnp.float32), precision=lax.Precision.HIGHEST)
        return (mean_group[:, None, :] + mixed).astype(jnp.bfloat16)
    result = lax.map(tile_analysis, (by_tile(block_ids), by_tile(live_mask), by_tile(observed), by_tile(state_pert), by_tile(state_mean)))
    return result.reshape(state_pert.shape)
```

```python
import functools

import jax
import jax.numpy as jnp
from jax import lax
from jax.experimental import pallas as pl
from jax.experimental.pallas import tpu as pltpu
from jax.sharding import PartitionSpec as P

MESH = pl.DeviceIdType.MESH
BF = jnp.bfloat16
F32 = jnp.float32
OBS = 4
POOL = 32
SLOTS = POOL + 1
CHUNKS = 8
PER = POOL // CHUNKS
GROUP = 8
OWN = 32
GROUPS = OWN // GROUP
HALF = GROUP // 2
COEF = (2.25, -2.4375, 1.6875, -0.5625, 0.0625)


def split(a):
    high = a.astype(BF)
    return high, (a - high.astype(F32)).astype(BF)


def product(left, right):
    left_high, left_low = left
    right_high, right_low = right
    row = jnp.concatenate([right_high, right_low], axis=1)
    both = jnp.dot(
        jnp.concatenate([left_high, left_low], axis=1),
        jnp.concatenate([row, row], axis=0),
        preferred_element_type=F32,
    )
    k = both.shape[1] // 2
    return both[:, :k] + both[:, k:]


def inverse_root(matrices, eye):
    every = range(len(matrices))
    w = list(matrices)
    w_parts = [split(a) for a in w]
    y, z = w_parts, None
    for step in range(6):
        if step:
            w = [product(z[i], y[i]) for i in every]
            w_parts = [split(a) for a in w]
        w2 = [product(a, a) for a in w_parts]
        tail = [split(COEF[3] * w[i] + COEF[4] * w2[i]) for i in every]
        w2_parts = [split(a) for a in w2]
        turn = [
            (COEF[0] * eye + COEF[1] * w[i]) + (COEF[2] * w2[i] + product(w2_parts[i], tail[i]))
            for i in every
        ]
        turn_parts = [split(a) for a in turn]
        if step < 5:
            y = [split(product(y[i], turn_parts[i])) for i in every]
        if step:
            z_full = [product(turn_parts[i], z[i]) for i in every]
            z = [split(a) for a in z_full]
        else:
            z = turn_parts
    return z_full, z


def solve_kernel(
    lists_ref, type_ref, prec_ref, weight_ref, innov_ref, pool_ref, out_ref,
    pool, rows, lists, index, gram, proj, mine,
    local_sem, small_send, small_recv, send, recv, pass_send, pass_recv,
    t_local, t_send, t_recv, tp_send, tp_recv,
):
    me = lax.axis_index("obs")
    right, left, far = lax.rem(me + 1, OBS), lax.rem(me + 3, OBS), lax.rem(me + 2, OBS)

    def remote(src, dst, send_sem, recv_sem, to):
        return pltpu.make_async_remote_copy(
            src_ref=src, dst_ref=dst, send_sem=send_sem, recv_sem=recv_sem,
            device_id={"obs": to}, device_id_type=MESH,
        )

    barrier = pltpu.get_barrier_semaphore()
    for other in (right, left, far):
        pl.semaphore_signal(barrier, inc=1, device_id={"obs": other}, device_id_type=MESH)

    keep = pltpu.make_async_copy(pool_ref, pool.at[me], local_sem)
    keep.start()
    for b in range(POOL):
        weighted = weight_ref[pl.ds(b, 1), :] * prec_ref[type_ref[b]]
        rows[me, pl.ds(b, 1), :] = weighted.astype(BF).astype(F32)
        rows[me, pl.ds(POOL + b, 1), :] = (weighted * innov_ref[pl.ds(b, 1), :]).astype(BF).astype(F32)
    lists[me] = lists_ref[...]
    eye = (
        lax.broadcasted_iota(jnp.int32, (128, 128), 0) == lax.broadcasted_iota(jnp.int32, (128, 128), 1)
    ).astype(F32)
    for o in range(OBS):
        gram[o * SLOTS + POOL] = jnp.zeros((128, 128), F32)
        proj[o, pl.ds(POOL, 8), :] = jnp.zeros((8, 128), F32)
    pl.semaphore_wait(barrier, 3)

    small = []
    for d, to in enumerate((right, left, far)):
        for j, ref in enumerate((rows, lists)):
            small.append(remote(ref.at[me], ref.at[me], small_send.at[d, j], small_recv.at[d, j], to))
            small[-1].start()

    def piece(o, k):
        return pool.at[o, pl.ds(k * PER, PER)]

    sends = []
    for k in range(CHUNKS):
        for d, to in enumerate((right, left)):
            sends.append(
                remote(pool_ref.at[pl.ds(k * PER, PER)], piece(me, k), send.at[d, k], recv.at[d, k], to)
            )
            sends[-1].start()

    def block_grams(o, k):
        for j in range(PER):
            b = k * PER + j
            pert = pool[o, b]
            weight = rows[o, pl.ds(b, 1), :]
            innov = rows[o, pl.ds(POOL + b, 1), :]
            scaled = (pert.astype(F32) * weight).astype(BF)
            lhs = jnp.concatenate([scaled, jnp.broadcast_to(innov, (16, 128)).astype(BF)], axis=0)
            res = lax.dot_general(lhs, pert, (((1,), (1,)), ((), ())), preferred_element_type=F32)
            gram[o * SLOTS + b] = res[:128]
            proj[o, pl.ds(b, 1), :] = res[128:129]

    keep.wait()

    def own_step(k, _):
        block_grams(me, k)
        return 0

    lax.fori_loop(0, CHUNKS, own_step, 0)
    for c in small:
        c.wait_recv()
    to_index = pltpu.make_async_copy(lists, index, local_sem)
    to_index.start()
    passes = []
    for k in range(CHUNKS):
        for d, source, to in ((0, left, right), (1, right, left)):
            remote(piece(source, k), piece(source, k), send.at[d, k], recv.at[d, k], to).wait_recv()
            if k % 2 == d:
                passes.append(
                    remote(piece(source, k), piece(source, k), pass_send.at[k], pass_recv.at[k], to)
                )
                passes[-1].start()
        block_grams(left, k)
        block_grams(right, k)
    to_index.wait()
    for k in range(CHUNKS):
        passes[k].wait_recv()
        block_grams(far, k)

    def t_piece(o, g, at, size):
        return out_ref.at[pl.ds(o * OWN + g * GROUP + at, size)]

    def t_first(g, d, to):
        return remote(
            mine.at[pl.ds(g * GROUP, GROUP)], t_piece(me, g, 0, GROUP), t_send.at[d, g], t_recv.at[d, g], to
        )

    def t_pass(g, d, source, to):
        return remote(
            t_piece(source, g, d * HALF, HALF), t_piece(source, g, d * HALF, HALF),
            tp_send.at[d, g], tp_recv.at[d, g], to,
        )

    def forward(g):
        for d, source, to in ((0, left, right), (1, right, left)):
            t_first(g, d, to).wait_recv()
            t_pass(g, d, source, to).start()

    def solve_group(g, _):
        matrices, norms, vectors = [], [], []
        for i in range(GROUP):
            c = me * OWN + g * GROUP + i
            total, vector = None, None
            for o in range(OBS):
                for m in range(2):
                    b = index[o, m, c]
                    one, row = gram[o * SLOTS + b], proj[o, pl.ds(b, 1), :]
                    total = one if total is None else total + one
                    vector = row if vector is None else vector + row
            matrix = eye + total * (1.0 / 127.0)
            square = jnp.sum(jnp.sum(matrix * matrix, axis=0, keepdims=True), axis=1, keepdims=True)
            scale = lax.rsqrt(square)
            matrices.append(matrix * scale)
            norms.append(scale)
            vectors.append(vector)
        full, parts = inverse_root(matrices, eye)
        for i in range(GROUP):
            row = jnp.broadcast_to(vectors[i] * (norms[i] * (1.0 / 127.0)), (16, 128))
            row = product(split(row), parts[i])
            row = product(split(row), parts[i])
            solved = full[i] * jnp.sqrt(norms[i]) + row[0:1]
            mine[g * GROUP + i] = solved.astype(BF)
        for d, to in ((0, right), (1, left)):
            t_first(g, d, to).start()
        pltpu.make_async_copy(
            mine.at[pl.ds(g * GROUP, GROUP)], t_piece(me, g, 0, GROUP), t_local.at[g]
        ).start()

        @pl.when(g > 0)
        def _():
            forward(g - 1)

        return 0

    lax.fori_loop(0, GROUPS, solve_group, 0)
    forward(GROUPS - 1)
    for g in range(GROUPS):
        for d, to in ((0, right), (1, left)):
            t_pass(g, d, far, to).wait_recv()
            t_pass(g, d, far, to).wait_send()
            t_first(g, d, to).wait_send()
        pltpu.make_async_copy(
            mine.at[pl.ds(g * GROUP, GROUP)], t_piece(me, g, 0, GROUP), t_local.at[g]
        ).wait()
    for c in small + sends + passes:
        c.wait_send()


APPLY = 8


def apply_kernel(count_ref, t_ref, x_ref, mean_ref, out_ref):
    count = count_ref[lax.axis_index("region")]
    step = pl.program_id(0)
    for i in range(APPLY):
        x = x_ref[i]
        mixed = jnp.dot(t_ref[i], x, preferred_element_type=F32)
        mixed = jnp.where(step * APPLY + i < count, mixed, x.astype(F32))
        out_ref[i] = (mixed + mean_ref[pl.ds(i, 1), :]).astype(BF)


def local(
    state_pert, state_mean, obs_pert, innov, obs_weight, block_type, type_prec, block_list, block_count, obs_clusters
):
    clusters, members, points = state_pert.shape
    live = jnp.arange(block_list.shape[1], dtype=jnp.int32)[None, :] < block_count
    lists = jnp.where(live, block_list, POOL).T
    lists = jnp.pad(lists, ((0, 8 - lists.shape[0]), (0, 0)))
    dma, regular = pltpu.SemaphoreType.DMA, pltpu.SemaphoreType.REGULAR
    vmem, smem = pl.BlockSpec(memory_space=pltpu.VMEM), pl.BlockSpec(memory_space=pltpu.SMEM)
    anywhere = pl.BlockSpec(memory_space=pl.ANY)
    transforms = pl.pallas_call(
        solve_kernel,
        out_shape=jax.ShapeDtypeStruct((clusters, members, members), BF),
        in_specs=[vmem, smem, smem, vmem, vmem, anywhere],
        out_specs=anywhere,
        scratch_shapes=[
            pltpu.VMEM((OBS, POOL, members, 128), BF),
            pltpu.VMEM((OBS, 2 * POOL, 128), F32),
            pltpu.VMEM((OBS, 8, clusters), jnp.int32),
            pltpu.SMEM((OBS, 8, clusters), jnp.int32),
            pltpu.VMEM((OBS * SLOTS, members, members), F32),
            pltpu.VMEM((OBS, POOL + 8, members), F32),
            pltpu.VMEM((OWN, members, members), BF),
            dma,
            dma((3, 2)), dma((3, 2)),
            dma((2, CHUNKS)), dma((2, CHUNKS)),
            dma((CHUNKS,)), dma((CHUNKS,)),
            dma((GROUPS,)),
            dma((2, GROUPS)), dma((2, GROUPS)),
            dma((2, GROUPS)), dma((2, GROUPS)),
        ],
        compiler_params=pltpu.CompilerParams(
            collective_id=0, has_side_effects=True, vmem_limit_bytes=40 << 20
        ),
        name="solve",
    )(lists, block_type, type_prec, obs_weight, innov, obs_pert)
    return pl.pallas_call(
        apply_kernel,
        grid=(clusters // APPLY,),
        out_shape=jax.ShapeDtypeStruct(state_pert.shape, BF),
        in_specs=[
            smem,
            pl.BlockSpec((APPLY, members, members), lambda s: (s, 0, 0)),
            pl.BlockSpec((APPLY, members, points), lambda s: (s, 0, 0)),
            pl.BlockSpec((APPLY, points), lambda s: (s, 0)),
        ],
        out_specs=pl.BlockSpec((APPLY, members, points), lambda s: (s, 0, 0)),
        compiler_params=pltpu.CompilerParams(vmem_limit_bytes=32 << 20),
        name="apply",
    )(obs_clusters, transforms, state_pert, state_mean)


def solution(mesh):
    placed = (
        P("region", None, "obs"),
        P("region", "obs"),
        P(("region", "obs"), None, None),
        P(("region", "obs"), None),
        P(("region", "obs"), None),
        P(("region", "obs")),
        P(),
        P("region", "obs"),
        P("region", "obs"),
        P(),
    )
    return jax.shard_map(
        local, mesh=mesh, in_specs=placed, out_specs=P("region", None, "obs"), check_vma=False
    )
```

```python
import functools

import jax
import jax.numpy as jnp
from jax import lax
from jax.experimental import pallas as pl
from jax.experimental.pallas import tpu as pltpu
from jax.sharding import PartitionSpec as P

MESH = pl.DeviceIdType.MESH
BF = jnp.bfloat16
F32 = jnp.float32
K = 128
OBS = 4
CORES = 2
POOL = 32
SLOTS = POOL + 1
CHUNKS = 8
PER = POOL // CHUNKS
GROUP = 8
OWN = 32
GROUPS = OWN // GROUP
UNIT = 4
UNITS = GROUP // UNIT
PACKED = UNIT // 2 * K + 16
COEF = (2.25, -2.4375, 1.6875, -0.5625, 0.0625)


def split(a):
    high = a.astype(BF)
    return high, (a - high.astype(F32)).astype(BF)


def product(left, right):
    left_high, left_low = left
    right_high, right_low = right
    row = jnp.concatenate([right_high, right_low], axis=1)
    both = jnp.dot(
        jnp.concatenate([left_high, left_low], axis=1),
        jnp.concatenate([row, row], axis=0),
        preferred_element_type=F32,
    )
    return both[:, :K] + both[:, K:]


def inverse_root(matrices, eye):
    every = range(len(matrices))
    w = list(matrices)
    w_parts = [split(a) for a in w]
    y, z = w_parts, None
    for step in range(6):
        if step:
            w = [product(z[i], y[i]) for i in every]
            w_parts = [split(a) for a in w]
        w2 = [product(a, a) for a in w_parts]
        tail = [split(COEF[3] * w[i] + COEF[4] * w2[i]) for i in every]
        w2_parts = [split(a) for a in w2]
        turn = [
            (COEF[0] * eye + COEF[1] * w[i]) + (COEF[2] * w2[i] + product(w2_parts[i], tail[i]))
            for i in every
        ]
        turn_parts = [split(a) for a in turn]
        if step < 5:
            y = [split(product(y[i], turn_parts[i])) for i in every]
        if step:
            z_full = [product(turn_parts[i], z[i]) for i in every]
            z = [split(a) for a in z_full]
        else:
            z = turn_parts
    return z_full, z


def places():
    rows = lax.broadcasted_iota(jnp.int32, (K, K), 0)
    columns = lax.broadcasted_iota(jnp.int32, (K, K), 1)
    return rows, columns


def solve_kernel(
    list_ref, count_ref, type_ref, prec_ref, weight_ref, innov_ref, pool_ref, out_ref,
    in_list, in_count, in_type, in_prec, in_weight, in_innov,
    pool, own_rows, own_lists, rows, lists, index, gram, proj, mine,
    in_sem, local_sem, small_send, small_recv, send, twin_send, recv,
    t_local, t_send, t_recv, f_send, f_recv,
):
    me, region = lax.axis_index("obs"), lax.axis_index("region")
    core = lax.rem(region, CORES)
    base = region - core
    twin = base + 1 - core
    partner, cross, far = me + 1 - 2 * lax.rem(me, 2), 3 - me, lax.rem(me + 2, OBS)
    tile = me // 2
    primary = core == tile
    solver = lax.rem(me, 2) * CORES + core

    def remote(src, dst, send_sem, recv_sem, to_region, to):
        return pltpu.make_async_remote_copy(
            src_ref=src, dst_ref=dst, send_sem=send_sem, recv_sem=recv_sem,
            device_id={"region": to_region, "obs": to}, device_id_type=MESH,
        )

    barrier = pltpu.get_barrier_semaphore()
    for other in range(1, OBS):
        for c in range(CORES):
            pl.semaphore_signal(
                barrier, inc=1, device_id={"region": base + c, "obs": lax.rem(me + other, OBS)}, device_id_type=MESH
            )
    pl.semaphore_signal(barrier, inc=1, device_id={"region": twin, "obs": me}, device_id_type=MESH)

    reads = []
    for j, (src, dst) in enumerate((
        (type_ref, in_type), (prec_ref, in_prec), (weight_ref, in_weight),
        (innov_ref, in_innov), (list_ref, in_list), (count_ref, in_count),
    )):
        reads.append(pltpu.make_async_copy(src, dst, in_sem.at[j]))
        reads[-1].start()
    for c in reads:
        c.wait()

    @pl.when(primary)
    def _():
        pltpu.make_async_copy(pool_ref, pool.at[me], local_sem).start()

    for b in range(POOL):
        weighted = in_weight[pl.ds(b, 1), :] * in_prec[in_type[b]]
        own_rows[pl.ds(b, 1), :] = weighted.astype(BF).astype(F32)
        own_rows[pl.ds(POOL + b, 1), :] = (weighted * in_innov[pl.ds(b, 1), :]).astype(BF).astype(F32)
    entry = lax.broadcasted_iota(jnp.int32, (2, K), 0)
    own_lists[...] = jnp.full((8, K), POOL, jnp.int32)
    own_lists[pl.ds(0, 2), :] = jnp.where(entry < in_count[...], in_list[...], POOL)
    place_row, place_column = places()
    eye = (place_row == place_column).astype(F32)
    for o in range(OBS):
        gram[o * SLOTS + POOL] = jnp.zeros((K, K), F32)
        proj[o, pl.ds(POOL, 8), :] = jnp.zeros((8, K), F32)
    pl.semaphore_wait(barrier, 7)

    def small(j, a, c):
        src, dst = ((own_rows, rows), (own_lists, lists))[j]
        return remote(src, dst.at[me], small_send.at[j, a, c], small_recv.at[j, me], base + c, 2 * core + a)

    def elsewhere(a, c):
        return jnp.logical_not(jnp.logical_and(primary, jnp.logical_and(2 * core + a == me, core == c)))

    for a in range(2):
        for c in range(CORES):
            @pl.when(elsewhere(a, c))
            def _():
                for j in range(2):
                    small(j, a, c).start()

    def piece(o, k):
        return pool.at[o, pl.ds(k * PER, PER)]

    def to_chip(src, o, k, to):
        return remote(src, piece(o, k), send.at[o, k], recv.at[o, k], region, to)

    def to_twin(src, o, k):
        return remote(src, piece(o, k), twin_send.at[o, k], recv.at[o, k], twin, me)

    def own_piece(k):
        return pool_ref.at[pl.ds(k * PER, PER)]

    @pl.when(primary)
    def _():
        def body(k, _):
            to_chip(own_piece(k), me, k, partner).start()
            to_twin(own_piece(k), me, k).start()
            return 0

        lax.fori_loop(0, CHUNKS, body, 0)
        rows[me] = own_rows[...]
        lists[me] = own_lists[...]

    @pl.when(jnp.logical_not(primary))
    def _():
        def body(k, _):
            to_chip(own_piece(k), me, k, cross).start()
            return 0

        lax.fori_loop(0, CHUNKS, body, 0)

    def arrived(o, k):
        to_twin(piece(o, k), o, k).wait_recv()

    def block_grams(o, k):
        for j in range(PER):
            b = k * PER + j
            pert = pool[o, b]
            weight = rows[o, pl.ds(b, 1), :]
            innov = rows[o, pl.ds(POOL + b, 1), :]
            scaled = (pert.astype(F32) * weight).astype(BF)
            lhs = jnp.concatenate([scaled, jnp.broadcast_to(innov, (16, K)).astype(BF)], axis=0)
            res = lax.dot_general(lhs, pert, (((1,), (1,)), ((), ())), preferred_element_type=F32)
            gram[o * SLOTS + b] = res[:K]
            proj[o, pl.ds(b, 1), :] = res[K:K + 1]

    def hand_on(k):
        @pl.when(k < CHUNKS)
        def _():
            arrived(cross, k)

            @pl.when(primary)
            def _():
                to_chip(piece(cross, k), cross, k, partner).start()
                to_twin(piece(cross, k), cross, k).start()

            arrived(partner, k)

            @pl.when(primary)
            def _():
                to_twin(piece(partner, k), partner, k).start()

        @pl.when(k >= 2)
        def _():
            arrived(far, k - 2)

            @pl.when(primary)
            def _():
                to_twin(piece(far, k - 2), far, k - 2).start()

    hand_on(0)
    hand_on(1)
    for o in range(OBS):
        @pl.when(jnp.logical_not(jnp.logical_and(primary, me == o)))
        def _():
            for j, (src, dst) in enumerate(((own_rows, rows), (own_lists, lists))):
                remote(src, dst.at[o], small_send.at[j, 0, 0], small_recv.at[j, o], twin, me).wait_recv()
    to_index = pltpu.make_async_copy(lists, index, in_sem.at[0])
    to_index.start()

    @pl.when(primary)
    def _():
        pltpu.make_async_copy(pool_ref, pool.at[me], local_sem).wait()

    def step(k, _):
        hand_on(k)

        @pl.when(jnp.logical_not(primary))
        def _():
            arrived(me, k - 2)

        for o in (me, cross, partner):
            block_grams(o, k - 2)

        @pl.when(k >= 3)
        def _():
            block_grams(far, k - 3)

        return 0

    lax.fori_loop(2, CHUNKS + 2, step, 0)
    block_grams(far, CHUNKS - 1)
    to_index.wait()

    def slot(of, g, unit, size):
        return out_ref.at[pl.ds(of * (OWN // UNIT) + g * UNITS + unit, size)]

    def unit_of(g, unit, size):
        return mine.at[pl.ds(g * UNITS + unit, size)]

    def t_first(j, of, g, unit, to):
        return remote(
            unit_of(g, unit, 1), slot(of, g, unit, 1), t_send.at[j, g, unit], t_recv.at[of, g, unit], base + tile, to
        )

    def t_keep(g):
        return pltpu.make_async_copy(unit_of(g, 0, UNITS), slot(solver, g, 0, UNITS), t_local.at[g])

    primary_int = primary.astype(jnp.int32)
    heard = primary_int * partner + (1 - primary_int) * cross
    onward = primary_int * cross + (1 - primary_int) * partner
    part = 1 - primary_int

    def t_pass(of, h, g, c, to):
        half = slot(of, g, h, 1)
        return remote(half, half, f_send.at[c, g], f_recv.at[of, h, g], region, to)

    def forward(g):
        for c in range(CORES):
            of = lax.rem(heard, 2) * CORES + c
            t_first(0, of, g, part, heard).wait_recv()
            t_pass(of, part, g, c, onward).start()

    upper = place_column >= place_row

    def solve_group(g, _):
        matrices, norms, vectors = [], [], []
        for i in range(GROUP):
            c = solver * OWN + g * GROUP + i
            total, vector = None, None
            for o in range(OBS):
                for m in range(2):
                    b = index[o, m, c]
                    one, row = gram[o * SLOTS + b], proj[o, pl.ds(b, 1), :]
                    total = one if total is None else total + one
                    vector = row if vector is None else vector + row
            matrix = eye + total * (1.0 / 127.0)
            square = jnp.sum(jnp.sum(matrix * matrix, axis=0, keepdims=True), axis=1, keepdims=True)
            scale = lax.rsqrt(square)
            matrices.append(matrix * scale)
            norms.append(scale)
            vectors.append(vector)
        full, parts = inverse_root(matrices, eye)
        for u in range(UNITS):
            extra = []
            for q in range(UNIT // 2):
                roots, means = [], []
                for i in (u * UNIT + 2 * q, u * UNIT + 2 * q + 1):
                    row = jnp.broadcast_to(vectors[i] * (norms[i] * (1.0 / 127.0)), (16, K))
                    row = product(split(row), parts[i])
                    row = product(split(row), parts[i])[0:1]
                    roots.append(full[i] * jnp.sqrt(norms[i]))
                    means += split(row)
                extra += [jnp.sum(roots[1] * eye, axis=0, keepdims=True).astype(BF)] + means
                mine[g * UNITS + u, pl.ds(q * K, K), :] = jnp.where(upper, roots[0], roots[1]).astype(BF)
            extra.append(jnp.zeros((16 - len(extra), K), BF))
            mine[g * UNITS + u, pl.ds(UNIT // 2 * K, 16), :] = jnp.concatenate(extra, axis=0)
        for j, unit, to in ((0, 0, partner), (1, 1, cross), (0, 1, partner), (1, 0, cross)):
            t_first(j, solver, g, unit, to).start()

        @pl.when(primary)
        def _():
            t_keep(g).start()

        @pl.when(jnp.logical_not(primary))
        def _():
            for unit in range(UNITS):
                t_first(2, solver, g, unit, me).start()

        @pl.when(g > 0)
        def _():
            forward(g - 1)

        return 0

    lax.fori_loop(0, GROUPS, solve_group, 0)
    forward(GROUPS - 1)

    @pl.when(primary)
    def _():
        for g in range(GROUPS):
            for unit in range(UNITS):
                t_first(2, lax.rem(me, 2) * CORES + 1 - core, g, unit, me).wait_recv()
            t_keep(g).wait()

        for k in range(CHUNKS):
            to_chip(own_piece(k), me, k, partner).wait_send()
            to_chip(piece(cross, k), cross, k, partner).wait_send()
            to_twin(own_piece(k), me, k).wait_send()
            for o in (cross, partner, far):
                to_twin(piece(o, k), o, k).wait_send()

    @pl.when(jnp.logical_not(primary))
    def _():
        for g in range(GROUPS):
            for c in range(CORES):
                of = lax.rem(far, 2) * CORES + c
                for h in range(2):
                    t_pass(of, h, g, c, onward).wait_recv()
            for unit in range(UNITS):
                t_first(2, solver, g, unit, me).wait_send()

        for k in range(CHUNKS):
            to_chip(own_piece(k), me, k, cross).wait_send()

    for g in range(GROUPS):
        for unit in range(UNITS):
            t_first(0, solver, g, unit, partner).wait_send()
            t_first(1, solver, g, unit, cross).wait_send()
        for c in range(CORES):
            of = lax.rem(heard, 2) * CORES + c
            t_first(0, of, g, 1 - part, heard).wait_recv()
            t_pass(of, part, g, c, onward).wait_send()
    for a in range(2):
        for c in range(CORES):
            @pl.when(elsewhere(a, c))
            def _():
                for j in range(2):
                    small(j, a, c).wait_send()


APPLY = 16


def apply_kernel(clusters, count_ref, packed_ref, x_ref, mean_ref, out_ref, packed_in, x_in, result, in_sem, out_sem):
    count = count_ref[lax.axis_index("region")]
    steps = clusters // APPLY

    def reads(s):
        here, units = pl.ds(s * APPLY, APPLY), pl.ds(s * (APPLY // UNIT), APPLY // UNIT)
        return (
            pltpu.make_async_copy(packed_ref.at[units], packed_in.at[units], in_sem.at[0, s]),
            pltpu.make_async_copy(x_ref.at[here], x_in.at[here], in_sem.at[1, s]),
        )

    def write(s):
        here = pl.ds(s * APPLY, APPLY)
        return pltpu.make_async_copy(result.at[here], out_ref.at[here], out_sem.at[s])

    for s in range(steps):
        for c in reads(s):
            c.start()
    place_row, place_column = places()
    diagonal, upper, lower = place_row == place_column, place_column >= place_row, place_column < place_row

    def body(s, _):
        for c in reads(s):
            c.wait()
        for u in range(APPLY // UNIT):
            unit = s * (APPLY // UNIT) + u
            extra = packed_in[unit, pl.ds(UNIT // 2 * K, 16), :].astype(F32)
            for q in range(UNIT // 2):
                packed = packed_in[unit, pl.ds(q * K, K), :]
                straight = packed.astype(F32)
                turned = straight.T
                roots = (
                    jnp.where(upper, straight, turned),
                    jnp.where(lower, straight, jnp.where(diagonal, extra[5 * q:5 * q + 1], turned)),
                )
                for i in range(2):
                    c = unit * UNIT + 2 * q + i
                    m = 5 * q + 1 + 2 * i
                    solved = (roots[i] + (extra[m:m + 1] + extra[m + 1:m + 2])).astype(BF)
                    x = x_in[c]
                    mixed = jnp.dot(solved, x, preferred_element_type=F32)
                    mixed = jnp.where(c < count, mixed, x.astype(F32))
                    result[c] = (mixed + mean_ref[pl.ds(c, 1), :]).astype(BF)
        write(s).start()
        return 0

    lax.fori_loop(0, steps, body, 0)
    for s in range(steps):
        write(s).wait()


def local(
    state_pert, state_mean, obs_pert, innov, obs_weight, block_type, type_prec, block_list, block_count, obs_clusters
):
    clusters, members, points = state_pert.shape
    dma = pltpu.SemaphoreType.DMA
    vmem, smem = pl.BlockSpec(memory_space=pltpu.VMEM), pl.BlockSpec(memory_space=pltpu.SMEM)
    hbm, anywhere = pl.BlockSpec(memory_space=pltpu.HBM), pl.BlockSpec(memory_space=pl.ANY)
    packed = pl.pallas_call(
        solve_kernel,
        out_shape=jax.ShapeDtypeStruct((clusters // UNIT, PACKED, members), BF),
        in_specs=[hbm] * 7,
        out_specs=anywhere,
        scratch_shapes=[
            pltpu.VMEM((2, clusters), jnp.int32),
            pltpu.VMEM((1, clusters), jnp.int32),
            pltpu.SMEM((POOL,), jnp.int32),
            pltpu.SMEM(type_prec.shape, F32),
            pltpu.VMEM((POOL, K), F32),
            pltpu.VMEM((POOL, K), F32),
            pltpu.VMEM((OBS, POOL, members, K), BF),
            pltpu.VMEM((2 * POOL, K), F32),
            pltpu.VMEM((8, clusters), jnp.int32),
            pltpu.VMEM((OBS, 2 * POOL, K), F32),
            pltpu.VMEM((OBS, 8, clusters), jnp.int32),
            pltpu.SMEM((OBS, 8, clusters), jnp.int32),
            pltpu.VMEM((OBS * SLOTS, members, members), F32),
            pltpu.VMEM((OBS, POOL + 8, members), F32),
            pltpu.VMEM((OWN // UNIT, PACKED, members), BF),
            dma((6,)), dma,
            dma((2, 2, CORES)), dma((2, OBS)),
            dma((OBS, CHUNKS)), dma((OBS, CHUNKS)), dma((OBS, CHUNKS)),
            dma((GROUPS,)),
            dma((3, GROUPS, UNITS)), dma((OBS, GROUPS, UNITS)),
            dma((CORES, GROUPS)), dma((OBS, 2, GROUPS)),
        ],
        compiler_params=pltpu.CompilerParams(
            collective_id=0, has_side_effects=True, vmem_limit_bytes=60 << 20
        ),
        name="solve",
    )(block_list.T, block_count.T, block_type, type_prec, obs_weight, innov, obs_pert)
    return pl.pallas_call(
        functools.partial(apply_kernel, clusters),
        out_shape=jax.ShapeDtypeStruct(state_pert.shape, BF),
        in_specs=[smem, hbm, hbm, vmem],
        out_specs=hbm,
        scratch_shapes=[
            pltpu.VMEM(packed.shape, BF), pltpu.VMEM(state_pert.shape, BF), pltpu.VMEM(state_pert.shape, BF),
            dma((2, clusters // APPLY)), dma((clusters // APPLY,)),
        ],
        compiler_params=pltpu.CompilerParams(vmem_limit_bytes=58 << 20),
        name="apply",
    )(obs_clusters, packed, state_pert, state_mean)


def solution(mesh):
    placed = (
        P("region", None, "obs"),
        P("region", "obs"),
        P(("region", "obs"), None, None),
        P(("region", "obs"), None),
        P(("region", "obs"), None),
        P(("region", "obs")),
        P(),
        P("region", "obs"),
        P("region", "obs"),
        P(),
    )
    return jax.shard_map(
        local, mesh=mesh, in_specs=placed, out_specs=P("region", None, "obs"), check_vma=False
    )
```

```python
import functools

import jax
import jax.numpy as jnp
from jax import lax
from jax.experimental import pallas as pl
from jax.experimental.pallas import tpu as pltpu
from jax.sharding import PartitionSpec as P

MESH = pl.DeviceIdType.MESH
BF = jnp.bfloat16
F32 = jnp.float32
K = 128
OBS = 4
CORES = 2
POOL = 32
SLOTS = POOL + 1
CHUNKS = 4
PER = POOL // CHUNKS
RELAYED = 1
DIRECT = CHUNKS - RELAYED
GROUP = 8
OWN = 32
GROUPS = OWN // GROUP
UNIT = 4
UNITS = GROUP // UNIT
PACKED = UNIT // 2 * K + 16


def split(a):
    high = a.astype(BF)
    return high, (a - high.astype(F32)).astype(BF)


def product(left, right):
    left_high, left_low = left
    right_high, right_low = right
    row = jnp.concatenate([right_high, right_low], axis=1)
    both = jnp.dot(
        jnp.concatenate([left_high, left_low], axis=1),
        jnp.concatenate([row, row], axis=0),
        preferred_element_type=F32,
    )
    return both[:, :K] + both[:, K:]


def inverse_root(matrices, eye):
    every = range(len(matrices))
    w = list(matrices)
    w_parts = [split(a) for a in w]
    y, z = w_parts, None
    for step in range(6):
        if step:
            w = [product(z[i], y[i]) for i in every]
            w_parts = [split(a) for a in w]
        inner = [split((product(w_parts[i], w_parts[i]) - 4.5 * w[i]) + 3.375 * eye) for i in every]
        turn = [
            (1 / 16) * product(inner[i], inner[i]) + ((24.609375 / 16) * eye - (8.625 / 16) * w[i]) for i in every
        ]
        turn_parts = [split(a) for a in turn]
        if step < 5:
            y = [split(product(y[i], turn_parts[i])) for i in every]
        if step:
            z_full = [product(turn_parts[i], z[i]) for i in every]
            z = [split(a) for a in z_full]
        else:
            z = turn_parts
    return z_full


def places():
    rows = lax.broadcasted_iota(jnp.int32, (K, K), 0)
    columns = lax.broadcasted_iota(jnp.int32, (K, K), 1)
    return rows, columns


def solve_kernel(
    list_ref, count_ref, type_ref, prec_ref, weight_ref, innov_ref, pool_ref, out_ref,
    in_list, in_count, in_type, in_prec, in_weight, in_innov,
    pool, own_rows, own_lists, rows, lists, index, gram, proj, mine, stop,
    in_sem, local_sem, small_send, small_recv, send, twin_send, recv, r_send, r_recv,
    t_local, t_send, t_recv, f_send, f_recv,
):
    at, region = lax.axis_index("obs"), lax.axis_index("region")
    core = lax.rem(region, CORES)
    base = region - core
    twin = base + 1 - core
    odd = lax.rem(region // CORES, 2)
    beside = region + CORES * (1 - 2 * odd)
    me = lax.rem(at + odd, OBS)
    partner, cross, far = me + 1 - 2 * lax.rem(me, 2), 3 - me, lax.rem(me + 2, OBS)
    tile = me // 2
    primary = core == tile
    solver = lax.rem(me, 2) * CORES + core

    me_beside = lax.rem(at + 1 - odd, OBS)
    relay = core == me_beside // 2
    partner_beside = me_beside + 1 - 2 * lax.rem(me_beside, 2)

    def place(number):
        return lax.rem(number - odd + OBS, OBS)

    def remote(src, dst, send_sem, recv_sem, to_region, to):
        return pltpu.make_async_remote_copy(
            src_ref=src, dst_ref=dst, send_sem=send_sem, recv_sem=recv_sem,
            device_id={"region": to_region, "obs": place(to)}, device_id_type=MESH,
        )

    barrier = pltpu.get_barrier_semaphore()
    for other in range(1, OBS):
        for c in range(CORES):
            pl.semaphore_signal(
                barrier, inc=1, device_id={"region": base + c, "obs": lax.rem(at + other, OBS)}, device_id_type=MESH
            )
    pl.semaphore_signal(barrier, inc=1, device_id={"region": twin, "obs": at}, device_id_type=MESH)
    for to in (me, partner, cross):
        pl.semaphore_signal(barrier, inc=1, device_id={"region": beside, "obs": place(to)}, device_id_type=MESH)

    reads = []
    for j, (src, dst) in enumerate((
        (type_ref, in_type), (prec_ref, in_prec), (weight_ref, in_weight),
        (innov_ref, in_innov), (list_ref, in_list), (count_ref, in_count),
    )):
        reads.append(pltpu.make_async_copy(src, dst, in_sem.at[j]))
        reads[-1].start()
    for c in reads:
        c.wait()

    @pl.when(primary)
    def _():
        pltpu.make_async_copy(pool_ref, pool.at[me], local_sem).start()

    for b in range(POOL):
        weighted = in_weight[pl.ds(b, 1), :] * in_prec[in_type[b]]
        own_rows[pl.ds(b, 1), :] = weighted.astype(BF).astype(F32)
        own_rows[pl.ds(POOL + b, 1), :] = (weighted * in_innov[pl.ds(b, 1), :]).astype(BF).astype(F32)
    entry = lax.broadcasted_iota(jnp.int32, (2, K), 0)
    own_lists[...] = jnp.full((8, K), POOL, jnp.int32)
    own_lists[pl.ds(0, 2), :] = jnp.where(entry < in_count[...], in_list[...], POOL)
    place_row, place_column = places()
    eye = (place_row == place_column).astype(F32)
    for o in range(OBS):
        gram[o * SLOTS + POOL] = jnp.zeros((K, K), F32)
        proj[o, pl.ds(POOL, 8), :] = jnp.zeros((8, K), F32)
    pl.semaphore_wait(barrier, 10)

    def small(j, a, c):
        src, dst = ((own_rows, rows), (own_lists, lists))[j]
        return remote(src, dst.at[me], small_send.at[j, a, c], small_recv.at[j, me], base + c, 2 * core + a)

    def elsewhere(a, c):
        return jnp.logical_not(jnp.logical_and(primary, jnp.logical_and(2 * core + a == me, core == c)))

    for a in range(2):
        for c in range(CORES):
            @pl.when(elsewhere(a, c))
            def _():
                for j in range(2):
                    small(j, a, c).start()

    def piece(o, k):
        return pool.at[o, pl.ds(k * PER, PER)]

    def to_chip(src, o, k, to):
        return remote(src, piece(o, k), send.at[o, k], recv.at[o, k], region, to)

    def to_twin(src, o, k):
        return remote(src, piece(o, k), twin_send.at[o, k], recv.at[o, k], twin, me)

    def own_piece(k):
        return pool_ref.at[pl.ds(k * PER, PER)]

    def relay_out(k):
        return remote(own_piece(DIRECT + k), stop.at[k], r_send.at[0, k], r_recv.at[k], beside, partner)

    def relay_back(k):
        block = piece(partner_beside, DIRECT + k)
        return remote(stop.at[k], block, r_send.at[1, k], recv.at[partner_beside, DIRECT + k], beside, me)

    @pl.when(primary)
    def _():
        for k in range(RELAYED):
            relay_out(k).start()

        def body(k, _):
            @pl.when(k < DIRECT)
            def _():
                to_chip(own_piece(k), me, k, partner).start()

            to_twin(own_piece(k), me, k).start()
            return 0

        lax.fori_loop(0, CHUNKS, body, 0)
        rows[me] = own_rows[...]
        lists[me] = own_lists[...]

    @pl.when(jnp.logical_not(primary))
    def _():
        def body(k, _):
            to_chip(own_piece(k), me, k, cross).start()
            return 0

        lax.fori_loop(0, CHUNKS, body, 0)

    def arrived(o, k):
        to_twin(piece(o, k), o, k).wait_recv()

    def block_grams(o, k):
        for j in range(PER):
            b = k * PER + j
            pert = pool[o, b]
            weight = rows[o, pl.ds(b, 1), :]
            innov = rows[o, pl.ds(POOL + b, 1), :]
            scaled = (pert.astype(F32) * weight).astype(BF)
            lhs = jnp.concatenate([scaled, jnp.broadcast_to(innov, (16, K)).astype(BF)], axis=0)
            res = lax.dot_general(lhs, pert, (((1,), (1,)), ((), ())), preferred_element_type=F32)
            gram[o * SLOTS + b] = res[:K]
            proj[o, pl.ds(b, 1), :] = res[K:K + 1]

    def hand_on(k):
        @pl.when(jnp.logical_and(relay, jnp.logical_and(k >= 1, k <= RELAYED)))
        def _():
            relay_out(k - 1).wait_recv()
            relay_back(k - 1).start()

        @pl.when(k < CHUNKS)
        def _():
            arrived(cross, k)

            @pl.when(primary)
            def _():
                to_chip(piece(cross, k), cross, k, partner).start()
                to_twin(piece(cross, k), cross, k).start()

            arrived(partner, k)

            @pl.when(primary)
            def _():
                to_twin(piece(partner, k), partner, k).start()

        @pl.when(k >= 2)
        def _():
            arrived(far, k - 2)

            @pl.when(primary)
            def _():
                to_twin(piece(far, k - 2), far, k - 2).start()

    hand_on(0)
    hand_on(1)
    for o in range(OBS):
        @pl.when(jnp.logical_not(jnp.logical_and(primary, me == o)))
        def _():
            for j, (src, dst) in enumerate(((own_rows, rows), (own_lists, lists))):
                remote(src, dst.at[o], small_send.at[j, 0, 0], small_recv.at[j, o], twin, me).wait_recv()
    to_index = pltpu.make_async_copy(lists, index, in_sem.at[0])
    to_index.start()

    @pl.when(primary)
    def _():
        pltpu.make_async_copy(pool_ref, pool.at[me], local_sem).wait()

    def grams(k):
        @pl.when(jnp.logical_not(primary))
        def _():
            arrived(me, k - 2)

        for o in (me, cross, partner):
            block_grams(o, k - 2)

        @pl.when(k >= 3)
        def _():
            block_grams(far, k - 3)

    def step(k, _):
        hand_on(k)
        grams(k)
        return 0

    def last_step(k, _):
        grams(k)
        hand_on(k)
        return 0

    lax.fori_loop(2, CHUNKS, step, 0)
    lax.fori_loop(CHUNKS, CHUNKS + 2, last_step, 0)
    block_grams(far, CHUNKS - 1)
    to_index.wait()

    def slot(of, g, unit, size):
        return out_ref.at[pl.ds(of * (OWN // UNIT) + g * UNITS + unit, size)]

    def unit_of(g, unit, size):
        return mine.at[pl.ds(g * UNITS + unit, size)]

    def t_first(j, of, g, unit, to):
        return remote(
            unit_of(g, unit, 1), slot(of, g, unit, 1), t_send.at[j, g, unit], t_recv.at[of, g, unit], base + tile, to
        )

    def t_keep(g):
        return pltpu.make_async_copy(unit_of(g, 0, UNITS), slot(solver, g, 0, UNITS), t_local.at[g])

    primary_int = primary.astype(jnp.int32)
    heard = primary_int * partner + (1 - primary_int) * cross
    onward = primary_int * cross + (1 - primary_int) * partner
    part = 1 - primary_int

    def t_pass(of, h, g, c, to):
        half = slot(of, g, h, 1)
        return remote(half, half, f_send.at[c, g], f_recv.at[of, h, g], region, to)

    def forward(g):
        for c in range(CORES):
            of = lax.rem(heard, 2) * CORES + c
            t_first(0, of, g, part, heard).wait_recv()
            t_pass(of, part, g, c, onward).start()

    upper = place_column >= place_row

    def solve_group(g, _):
        matrices, norms, vectors = [], [], []
        for i in range(GROUP):
            c = solver * OWN + g * GROUP + i
            total, vector = None, None
            for o in range(OBS):
                for m in range(2):
                    b = index[o, m, c]
                    one, row = gram[o * SLOTS + b], proj[o, pl.ds(b, 1), :]
                    total = one if total is None else total + one
                    vector = row if vector is None else vector + row
            matrix = eye + total * (1.0 / 127.0)
            square = jnp.sum(jnp.sum(matrix * matrix, axis=0, keepdims=True), axis=1, keepdims=True)
            scale = lax.rsqrt(square)
            matrices.append(matrix * scale)
            norms.append(scale)
            vectors.append(vector)
        full = inverse_root(matrices, eye)
        for u in range(UNITS):
            extra = []
            for q in range(UNIT // 2):
                roots, means = [], []
                for i in (u * UNIT + 2 * q, u * UNIT + 2 * q + 1):
                    row = vectors[i] * (norms[i] * (1.0 / 127.0))
                    column = jnp.sum(full[i] * row, axis=1, keepdims=True)
                    row = jnp.sum(full[i] * column, axis=0, keepdims=True)
                    roots.append(full[i] * jnp.sqrt(norms[i]))
                    means += split(row)
                extra += [jnp.sum(roots[1] * eye, axis=0, keepdims=True).astype(BF)] + means
                mine[g * UNITS + u, pl.ds(q * K, K), :] = jnp.where(upper, roots[0], roots[1]).astype(BF)
            extra.append(jnp.zeros((16 - len(extra), K), BF))
            mine[g * UNITS + u, pl.ds(UNIT // 2 * K, 16), :] = jnp.concatenate(extra, axis=0)
        for j, unit, to in ((0, 0, partner), (1, 1, cross), (0, 1, partner), (1, 0, cross)):
            t_first(j, solver, g, unit, to).start()

        @pl.when(primary)
        def _():
            t_keep(g).start()

        @pl.when(jnp.logical_not(primary))
        def _():
            for unit in range(UNITS):
                t_first(2, solver, g, unit, me).start()

        @pl.when(g > 0)
        def _():
            forward(g - 1)

        return 0

    lax.fori_loop(0, GROUPS, solve_group, 0)
    forward(GROUPS - 1)

    @pl.when(primary)
    def _():
        for g in range(GROUPS):
            for unit in range(UNITS):
                t_first(2, lax.rem(me, 2) * CORES + 1 - core, g, unit, me).wait_recv()
            t_keep(g).wait()

        for k in range(DIRECT):
            to_chip(own_piece(k), me, k, partner).wait_send()
        for k in range(RELAYED):
            relay_out(k).wait_send()
        for k in range(CHUNKS):
            to_chip(piece(cross, k), cross, k, partner).wait_send()
            to_twin(own_piece(k), me, k).wait_send()
            for o in (cross, partner, far):
                to_twin(piece(o, k), o, k).wait_send()

    @pl.when(jnp.logical_not(primary))
    def _():
        for g in range(GROUPS):
            for c in range(CORES):
                of = lax.rem(far, 2) * CORES + c
                for h in range(2):
                    t_pass(of, h, g, c, onward).wait_recv()
            for unit in range(UNITS):
                t_first(2, solver, g, unit, me).wait_send()

        for k in range(CHUNKS):
            to_chip(own_piece(k), me, k, cross).wait_send()

    for g in range(GROUPS):
        for unit in range(UNITS):
            t_first(0, solver, g, unit, partner).wait_send()
            t_first(1, solver, g, unit, cross).wait_send()
        for c in range(CORES):
            of = lax.rem(heard, 2) * CORES + c
            t_first(0, of, g, 1 - part, heard).wait_recv()
            t_pass(of, part, g, c, onward).wait_send()
    @pl.when(relay)
    def _():
        for k in range(RELAYED):
            relay_back(k).wait_send()

    for a in range(2):
        for c in range(CORES):
            @pl.when(elsewhere(a, c))
            def _():
                for j in range(2):
                    small(j, a, c).wait_send()


APPLY = 16


def apply_kernel(clusters, count_ref, packed_ref, x_ref, mean_ref, out_ref, counts, packed_in, x_in, mean, result, in_sem, out_sem):
    steps = clusters // APPLY

    def reads(s):
        here, units = pl.ds(s * APPLY, APPLY), pl.ds(s * (APPLY // UNIT), APPLY // UNIT)
        return (
            pltpu.make_async_copy(packed_ref.at[units], packed_in.at[units], in_sem.at[0, s]),
            pltpu.make_async_copy(x_ref.at[here], x_in.at[here], in_sem.at[1, s]),
        )

    def write(s):
        here = pl.ds(s * APPLY, APPLY)
        return pltpu.make_async_copy(result.at[here], out_ref.at[here], out_sem.at[s])

    small = (
        pltpu.make_async_copy(count_ref, counts, in_sem.at[0, steps]),
        pltpu.make_async_copy(mean_ref, mean, in_sem.at[1, steps]),
    )
    for c in reads(0) + small:
        c.start()
    for s in range(1, steps):
        for c in reads(s):
            c.start()
    place_row, place_column = places()
    diagonal, upper, lower = place_row == place_column, place_column >= place_row, place_column < place_row

    eye = diagonal.astype(BF)
    for c in small:
        c.wait()
    count = counts[lax.axis_index("region")]

    def body(s, _):
        for c in reads(s):
            c.wait()
        for u in range(APPLY // UNIT):
            unit = s * (APPLY // UNIT) + u
            extra = packed_in[unit, pl.ds(UNIT // 2 * K, 16), :].astype(F32)
            for q in range(UNIT // 2):
                packed = packed_in[unit, pl.ds(q * K, K), :]
                straight = packed.astype(F32)
                turned = straight.T
                roots = (
                    jnp.where(upper, straight, turned),
                    jnp.where(lower, straight, jnp.where(diagonal, extra[5 * q:5 * q + 1], turned)),
                )
                for i in range(2):
                    c = unit * UNIT + 2 * q + i
                    m = 5 * q + 1 + 2 * i
                    solved = (roots[i] + (extra[m:m + 1] + extra[m + 1:m + 2])).astype(BF)
                    solved = jnp.where(c < count, solved, eye)
                    mixed = jnp.dot(solved, x_in[c], preferred_element_type=F32)
                    result[c] = (mixed + mean[pl.ds(c, 1), :]).astype(BF)
        write(s).start()
        return 0

    lax.fori_loop(0, steps, body, 0)
    for s in range(steps):
        write(s).wait()


def local(
    state_pert, state_mean, obs_pert, innov, obs_weight, block_type, type_prec, block_list, block_count, obs_clusters
):
    clusters, members, points = state_pert.shape
    dma = pltpu.SemaphoreType.DMA
    hbm, anywhere = pl.BlockSpec(memory_space=pltpu.HBM), pl.BlockSpec(memory_space=pl.ANY)
    packed = pl.pallas_call(
        solve_kernel,
        out_shape=jax.ShapeDtypeStruct((clusters // UNIT, PACKED, members), BF),
        in_specs=[hbm] * 7,
        out_specs=anywhere,
        scratch_shapes=[
            pltpu.VMEM((2, clusters), jnp.int32),
            pltpu.VMEM((1, clusters), jnp.int32),
            pltpu.SMEM((POOL,), jnp.int32),
            pltpu.SMEM(type_prec.shape, F32),
            pltpu.VMEM((POOL, K), F32),
            pltpu.VMEM((POOL, K), F32),
            pltpu.VMEM((OBS, POOL, members, K), BF),
            pltpu.VMEM((2 * POOL, K), F32),
            pltpu.VMEM((8, clusters), jnp.int32),
            pltpu.VMEM((OBS, 2 * POOL, K), F32),
            pltpu.VMEM((OBS, 8, clusters), jnp.int32),
            pltpu.SMEM((OBS, 8, clusters), jnp.int32),
            pltpu.VMEM((OBS * SLOTS, members, members), F32),
            pltpu.VMEM((OBS, POOL + 8, members), F32),
            pltpu.VMEM((OWN // UNIT, PACKED, members), BF),
            pltpu.VMEM((RELAYED, PER, members, K), BF),
            dma((6,)), dma,
            dma((2, 2, CORES)), dma((2, OBS)),
            dma((OBS, CHUNKS)), dma((OBS, CHUNKS)), dma((OBS, CHUNKS)),
            dma((2, RELAYED)), dma((RELAYED,)),
            dma((GROUPS,)),
            dma((3, GROUPS, UNITS)), dma((OBS, GROUPS, UNITS)),
            dma((CORES, GROUPS)), dma((OBS, 2, GROUPS)),
        ],
        compiler_params=pltpu.CompilerParams(
            collective_id=0, has_side_effects=True, vmem_limit_bytes=60 << 20
        ),
        name="solve",
    )(block_list.T, block_count.T, block_type, type_prec, obs_weight, innov, obs_pert)
    return pl.pallas_call(
        functools.partial(apply_kernel, clusters),
        out_shape=jax.ShapeDtypeStruct(state_pert.shape, BF),
        in_specs=[hbm] * 4,
        out_specs=hbm,
        scratch_shapes=[
            pltpu.SMEM(obs_clusters.shape, jnp.int32),
            pltpu.VMEM(packed.shape, BF), pltpu.VMEM(state_pert.shape, BF),
            pltpu.VMEM(state_mean.shape, F32), pltpu.VMEM(state_pert.shape, BF),
            dma((2, clusters // APPLY + 1)), dma((clusters // APPLY,)),
        ],
        compiler_params=pltpu.CompilerParams(vmem_limit_bytes=58 << 20),
        name="apply",
    )(obs_clusters, packed, state_pert, state_mean)


def solution(mesh):
    placed = (
        P("region", None, "obs"),
        P("region", "obs"),
        P(("region", "obs"), None, None),
        P(("region", "obs"), None),
        P(("region", "obs"), None),
        P(("region", "obs")),
        P(),
        P("region", "obs"),
        P("region", "obs"),
        P(),
    )
    return jax.shard_map(
        local, mesh=mesh, in_specs=placed, out_specs=P("region", None, "obs"), check_vma=False
    )
```

```python
import functools

import jax
import jax.numpy as jnp
from jax import lax
from jax.experimental import pallas as pl
from jax.experimental.pallas import tpu as pltpu
from jax.sharding import PartitionSpec as P

MESH = pl.DeviceIdType.MESH
BF = jnp.bfloat16
F32 = jnp.float32
K = 128
OBS = 4
CORES = 2
POOL = 32
SLOTS = POOL + 1
CHUNKS = 4
PER = POOL // CHUNKS
RELAYED = 1
DIRECT = CHUNKS - RELAYED
GROUP = 8
OWN = 32
GROUPS = OWN // GROUP
UNIT = 4
UNITS = GROUP // UNIT
PACKED = UNIT // 2 * K + 16


def split(a):
    high = a.astype(BF)
    return high, (a - high.astype(F32)).astype(BF)


def product(left, right):
    left_high, left_low = left
    right_high, right_low = right
    row = jnp.concatenate([right_high, right_low], axis=1)
    both = jnp.dot(
        jnp.concatenate([left_high, left_low], axis=1),
        jnp.concatenate([row, row], axis=0),
        preferred_element_type=F32,
    )
    return both[:, :K] + both[:, K:]


def root_stages(matrix, eye, result):
    w, w_parts = matrix, split(matrix)
    y, z = w_parts, None
    for step in range(6):
        if step:
            w = product(z, y)
            yield
            w_parts = split(w)
        inner = (product(w_parts, w_parts) - 4.5 * w) + 3.375 * eye
        yield
        inner = split(inner)
        turn = (1 / 16) * product(inner, inner) + ((24.609375 / 16) * eye - (8.625 / 16) * w)
        yield
        turn = split(turn)
        if step < 5:
            y = split(product(y, turn))
        if step:
            full = product(turn, z)
            z = split(full)
        else:
            z = turn
        yield
    result.append(full)


def inverse_root(matrices, eye):
    results = [[] for _ in matrices]
    live = [root_stages(matrix, eye, result) for matrix, result in zip(matrices, results)]
    for ahead in live[::2]:
        next(ahead)
    while live:
        live = [stages for stages in live if next(stages, True) is None]
    return [result[0] for result in results]


def places():
    rows = lax.broadcasted_iota(jnp.int32, (K, K), 0)
    columns = lax.broadcasted_iota(jnp.int32, (K, K), 1)
    return rows, columns


def solve_kernel(
    list_ref, count_ref, type_ref, prec_ref, weight_ref, innov_ref, pool_ref, out_ref,
    in_list, in_count, in_type, in_prec, in_weight, in_innov,
    pool, own_rows, own_lists, rows, lists, index, gram, proj, mine, stop,
    in_sem, local_sem, small_send, small_recv, send, twin_send, recv, r_send, r_recv,
    t_local, t_send, t_recv, f_send, f_recv,
):
    at, region = lax.axis_index("obs"), lax.axis_index("region")
    core = lax.rem(region, CORES)
    base = region - core
    twin = base + 1 - core
    odd = lax.rem(region // CORES, 2)
    beside = region + CORES * (1 - 2 * odd)
    me = lax.rem(at + odd, OBS)
    partner, cross, far = me + 1 - 2 * lax.rem(me, 2), 3 - me, lax.rem(me + 2, OBS)
    tile = me // 2
    primary = core == tile
    solver = lax.rem(me, 2) * CORES + core

    me_beside = lax.rem(at + 1 - odd, OBS)
    relay = core == me_beside // 2
    partner_beside = me_beside + 1 - 2 * lax.rem(me_beside, 2)

    def place(number):
        return lax.rem(number - odd + OBS, OBS)

    def remote(src, dst, send_sem, recv_sem, to_region, to):
        return pltpu.make_async_remote_copy(
            src_ref=src, dst_ref=dst, send_sem=send_sem, recv_sem=recv_sem,
            device_id={"region": to_region, "obs": place(to)}, device_id_type=MESH,
        )

    barrier = pltpu.get_barrier_semaphore()
    for other in range(1, OBS):
        for c in range(CORES):
            pl.semaphore_signal(
                barrier, inc=1, device_id={"region": base + c, "obs": lax.rem(at + other, OBS)}, device_id_type=MESH
            )
    pl.semaphore_signal(barrier, inc=1, device_id={"region": twin, "obs": at}, device_id_type=MESH)
    for to in (me, partner, cross):
        pl.semaphore_signal(barrier, inc=1, device_id={"region": beside, "obs": place(to)}, device_id_type=MESH)

    reads = []
    for j, (src, dst) in enumerate((
        (type_ref, in_type), (prec_ref, in_prec), (weight_ref, in_weight),
        (innov_ref, in_innov), (list_ref, in_list), (count_ref, in_count),
    )):
        reads.append(pltpu.make_async_copy(src, dst, in_sem.at[j]))
        reads[-1].start()
    for c in reads:
        c.wait()

    @pl.when(primary)
    def _():
        pltpu.make_async_copy(pool_ref, pool.at[me], local_sem).start()

    for b in range(POOL):
        weighted = in_weight[pl.ds(b, 1), :] * in_prec[in_type[b]]
        own_rows[pl.ds(b, 1), :] = weighted.astype(BF).astype(F32)
        own_rows[pl.ds(POOL + b, 1), :] = (weighted * in_innov[pl.ds(b, 1), :]).astype(BF).astype(F32)
    entry = lax.broadcasted_iota(jnp.int32, (2, K), 0)
    own_lists[...] = jnp.full((8, K), POOL, jnp.int32)
    own_lists[pl.ds(0, 2), :] = jnp.where(entry < in_count[...], in_list[...], POOL)
    place_row, place_column = places()
    eye = (place_row == place_column).astype(F32)
    for o in range(OBS):
        gram[o * SLOTS + POOL] = jnp.zeros((K, K), F32)
        proj[o, pl.ds(POOL, 8), :] = jnp.zeros((8, K), F32)
    pl.semaphore_wait(barrier, 10)

    def small(j, a, c):
        src, dst = ((own_rows, rows), (own_lists, lists))[j]
        return remote(src, dst.at[me], small_send.at[j, a, c], small_recv.at[j, me], base + c, 2 * core + a)

    def elsewhere(a, c):
        return jnp.logical_not(jnp.logical_and(primary, jnp.logical_and(2 * core + a == me, core == c)))

    for a in range(2):
        for c in range(CORES):
            @pl.when(elsewhere(a, c))
            def _():
                for j in range(2):
                    small(j, a, c).start()

    def piece(o, k):
        return pool.at[o, pl.ds(k * PER, PER)]

    def to_chip(src, o, k, to):
        return remote(src, piece(o, k), send.at[o, k], recv.at[o, k], region, to)

    def to_twin(src, o, k):
        return remote(src, piece(o, k), twin_send.at[o, k], recv.at[o, k], twin, me)

    def own_piece(k):
        return pool_ref.at[pl.ds(k * PER, PER)]

    def relay_out(k):
        return remote(own_piece(DIRECT + k), stop.at[k], r_send.at[0, k], r_recv.at[k], beside, partner)

    def relay_back(k):
        block = piece(partner_beside, DIRECT + k)
        return remote(stop.at[k], block, r_send.at[1, k], recv.at[partner_beside, DIRECT + k], beside, me)

    @pl.when(primary)
    def _():
        for k in range(RELAYED):
            relay_out(k).start()

        def body(k, _):
            @pl.when(k < DIRECT)
            def _():
                to_chip(own_piece(k), me, k, partner).start()

            to_twin(own_piece(k), me, k).start()
            return 0

        lax.fori_loop(0, CHUNKS, body, 0)
        rows[me] = own_rows[...]
        lists[me] = own_lists[...]

    @pl.when(jnp.logical_not(primary))
    def _():
        def body(k, _):
            to_chip(own_piece(k), me, k, cross).start()
            return 0

        lax.fori_loop(0, CHUNKS, body, 0)

    def arrived(o, k):
        to_twin(piece(o, k), o, k).wait_recv()

    def block_grams(o, k):
        for j in range(PER):
            b = k * PER + j
            pert = pool[o, b]
            weight = rows[o, pl.ds(b, 1), :]
            innov = rows[o, pl.ds(POOL + b, 1), :]
            scaled = (pert.astype(F32) * weight).astype(BF)
            lhs = jnp.concatenate([scaled, jnp.broadcast_to(innov, (16, K)).astype(BF)], axis=0)
            res = lax.dot_general(lhs, pert, (((1,), (1,)), ((), ())), preferred_element_type=F32)
            gram[o * SLOTS + b] = res[:K]
            proj[o, pl.ds(b, 1), :] = res[K:K + 1]

    def hand_on(k):
        @pl.when(jnp.logical_and(relay, jnp.logical_and(k >= 1, k <= RELAYED)))
        def _():
            relay_out(k - 1).wait_recv()
            relay_back(k - 1).start()

        @pl.when(k < CHUNKS)
        def _():
            arrived(cross, k)

            @pl.when(primary)
            def _():
                to_chip(piece(cross, k), cross, k, partner).start()
                to_twin(piece(cross, k), cross, k).start()

            arrived(partner, k)

            @pl.when(primary)
            def _():
                to_twin(piece(partner, k), partner, k).start()

        @pl.when(k >= 2)
        def _():
            arrived(far, k - 2)

            @pl.when(primary)
            def _():
                to_twin(piece(far, k - 2), far, k - 2).start()

    hand_on(0)
    hand_on(1)
    for o in range(OBS):
        @pl.when(jnp.logical_not(jnp.logical_and(primary, me == o)))
        def _():
            for j, (src, dst) in enumerate(((own_rows, rows), (own_lists, lists))):
                remote(src, dst.at[o], small_send.at[j, 0, 0], small_recv.at[j, o], twin, me).wait_recv()
    to_index = pltpu.make_async_copy(lists, index, in_sem.at[0])
    to_index.start()

    @pl.when(primary)
    def _():
        pltpu.make_async_copy(pool_ref, pool.at[me], local_sem).wait()

    def grams(k):
        @pl.when(jnp.logical_not(primary))
        def _():
            arrived(me, k - 2)

        for o in (me, cross, partner):
            block_grams(o, k - 2)

        @pl.when(k >= 3)
        def _():
            block_grams(far, k - 3)

    def step(k, _):
        hand_on(k)
        grams(k)
        return 0

    def last_step(k, _):
        grams(k)
        hand_on(k)
        return 0

    lax.fori_loop(2, CHUNKS, step, 0)
    lax.fori_loop(CHUNKS, CHUNKS + 2, last_step, 0)
    block_grams(far, CHUNKS - 1)
    to_index.wait()

    def slot(of, g, unit, size):
        return out_ref.at[pl.ds(of * (OWN // UNIT) + g * UNITS + unit, size)]

    def unit_of(g, unit, size):
        return mine.at[pl.ds(g * UNITS + unit, size)]

    def t_first(j, of, g, unit, to):
        return remote(
            unit_of(g, unit, 1), slot(of, g, unit, 1), t_send.at[j, g, unit], t_recv.at[of, g, unit], base + tile, to
        )

    def t_keep(g):
        return pltpu.make_async_copy(unit_of(g, 0, UNITS), slot(solver, g, 0, UNITS), t_local.at[g])

    primary_int = primary.astype(jnp.int32)
    heard = primary_int * partner + (1 - primary_int) * cross
    onward = primary_int * cross + (1 - primary_int) * partner
    part = 1 - primary_int

    def t_pass(of, h, g, c, to):
        half = slot(of, g, h, 1)
        return remote(half, half, f_send.at[c, g], f_recv.at[of, h, g], region, to)

    def forward(g):
        for c in range(CORES):
            of = lax.rem(heard, 2) * CORES + c
            t_first(0, of, g, part, heard).wait_recv()
            t_pass(of, part, g, c, onward).start()

    upper = place_column >= place_row

    def solve_group(g, _):
        matrices, norms, vectors = [], [], []
        for i in range(GROUP):
            c = solver * OWN + g * GROUP + i
            total, vector = None, None
            for o in range(OBS):
                for m in range(2):
                    b = index[o, m, c]
                    one, row = gram[o * SLOTS + b], proj[o, pl.ds(b, 1), :]
                    total = one if total is None else total + one
                    vector = row if vector is None else vector + row
            matrix = eye + total * (1.0 / 127.0)
            square = jnp.sum(jnp.sum(matrix * matrix, axis=0, keepdims=True), axis=1, keepdims=True)
            scale = lax.rsqrt(square)
            matrices.append(matrix * scale)
            norms.append(scale)
            vectors.append(vector)
        full = inverse_root(matrices, eye)
        for u in range(UNITS):
            extra = []
            for q in range(UNIT // 2):
                roots, means = [], []
                for i in (u * UNIT + 2 * q, u * UNIT + 2 * q + 1):
                    row = vectors[i] * (norms[i] * (1.0 / 127.0))
                    column = jnp.sum(full[i] * row, axis=1, keepdims=True)
                    row = jnp.sum(full[i] * column, axis=0, keepdims=True)
                    roots.append(full[i] * jnp.sqrt(norms[i]))
                    means += split(row)
                extra += [jnp.sum(roots[1] * eye, axis=0, keepdims=True).astype(BF)] + means
                mine[g * UNITS + u, pl.ds(q * K, K), :] = jnp.where(upper, roots[0], roots[1]).astype(BF)
            extra.append(jnp.zeros((16 - len(extra), K), BF))
            mine[g * UNITS + u, pl.ds(UNIT // 2 * K, 16), :] = jnp.concatenate(extra, axis=0)
        for j, unit, to in ((0, 0, partner), (1, 1, cross), (0, 1, partner), (1, 0, cross)):
            t_first(j, solver, g, unit, to).start()

        @pl.when(primary)
        def _():
            t_keep(g).start()

        @pl.when(jnp.logical_not(primary))
        def _():
            for unit in range(UNITS):
                t_first(2, solver, g, unit, me).start()

        @pl.when(g > 0)
        def _():
            forward(g - 1)

        return 0

    lax.fori_loop(0, GROUPS, solve_group, 0)
    forward(GROUPS - 1)

    @pl.when(primary)
    def _():
        for g in range(GROUPS):
            for unit in range(UNITS):
                t_first(2, lax.rem(me, 2) * CORES + 1 - core, g, unit, me).wait_recv()
            t_keep(g).wait()

        for k in range(DIRECT):
            to_chip(own_piece(k), me, k, partner).wait_send()
        for k in range(RELAYED):
            relay_out(k).wait_send()
        for k in range(CHUNKS):
            to_chip(piece(cross, k), cross, k, partner).wait_send()
            to_twin(own_piece(k), me, k).wait_send()
            for o in (cross, partner, far):
                to_twin(piece(o, k), o, k).wait_send()

    @pl.when(jnp.logical_not(primary))
    def _():
        for g in range(GROUPS):
            for c in range(CORES):
                of = lax.rem(far, 2) * CORES + c
                for h in range(2):
                    t_pass(of, h, g, c, onward).wait_recv()
            for unit in range(UNITS):
                t_first(2, solver, g, unit, me).wait_send()

        for k in range(CHUNKS):
            to_chip(own_piece(k), me, k, cross).wait_send()

    for g in range(GROUPS):
        for unit in range(UNITS):
            t_first(0, solver, g, unit, partner).wait_send()
            t_first(1, solver, g, unit, cross).wait_send()
        for c in range(CORES):
            of = lax.rem(heard, 2) * CORES + c
            t_first(0, of, g, 1 - part, heard).wait_recv()
            t_pass(of, part, g, c, onward).wait_send()
    @pl.when(relay)
    def _():
        for k in range(RELAYED):
            relay_back(k).wait_send()

    for a in range(2):
        for c in range(CORES):
            @pl.when(elsewhere(a, c))
            def _():
                for j in range(2):
                    small(j, a, c).wait_send()


APPLY = 32


def apply_kernel(clusters, count_ref, packed_ref, x_ref, mean_ref, out_ref, counts, packed_in, x_in, mean, result, in_sem, out_sem):
    steps = clusters // APPLY

    def reads(s):
        here, units = pl.ds(s * APPLY, APPLY), pl.ds(s * (APPLY // UNIT), APPLY // UNIT)
        return (
            pltpu.make_async_copy(packed_ref.at[units], packed_in.at[units], in_sem.at[0, s]),
            pltpu.make_async_copy(x_ref.at[here], x_in.at[here], in_sem.at[1, s]),
        )

    def write(s):
        here = pl.ds(s * APPLY, APPLY)
        return pltpu.make_async_copy(result.at[here], out_ref.at[here], out_sem.at[s])

    small = (
        pltpu.make_async_copy(count_ref, counts, in_sem.at[0, steps]),
        pltpu.make_async_copy(mean_ref, mean, in_sem.at[1, steps]),
    )
    for c in reads(0) + small:
        c.start()
    for s in range(1, steps):
        for c in reads(s):
            c.start()
    place_row, place_column = places()
    diagonal, upper, lower = place_row == place_column, place_column >= place_row, place_column < place_row

    eye = diagonal.astype(BF)
    for c in small:
        c.wait()
    count = counts[lax.axis_index("region")]

    def body(s, _):
        for c in reads(s):
            c.wait()
        for u in range(APPLY // UNIT):
            unit = s * (APPLY // UNIT) + u
            extra = packed_in[unit, pl.ds(UNIT // 2 * K, 16), :].astype(F32)
            for q in range(UNIT // 2):
                packed = packed_in[unit, pl.ds(q * K, K), :]
                straight = packed.astype(F32)
                turned = straight.T
                roots = (
                    jnp.where(upper, straight, turned),
                    jnp.where(lower, straight, jnp.where(diagonal, extra[5 * q:5 * q + 1], turned)),
                )
                for i in range(2):
                    c = unit * UNIT + 2 * q + i
                    m = 5 * q + 1 + 2 * i
                    solved = (roots[i] + (extra[m:m + 1] + extra[m + 1:m + 2])).astype(BF)
                    solved = jnp.where(c < count, solved, eye)
                    mixed = jnp.dot(solved, x_in[c], preferred_element_type=F32)
                    result[c] = (mixed + mean[pl.ds(c, 1), :]).astype(BF)
        write(s).start()
        return 0

    lax.fori_loop(0, steps, body, 0)
    for s in range(steps):
        write(s).wait()


def local(
    state_pert, state_mean, obs_pert, innov, obs_weight, block_type, type_prec, block_list, block_count, obs_clusters
):
    clusters, members, points = state_pert.shape
    dma = pltpu.SemaphoreType.DMA
    hbm, anywhere = pl.BlockSpec(memory_space=pltpu.HBM), pl.BlockSpec(memory_space=pl.ANY)
    packed = pl.pallas_call(
        solve_kernel,
        out_shape=jax.ShapeDtypeStruct((clusters // UNIT, PACKED, members), BF),
        in_specs=[hbm] * 7,
        out_specs=anywhere,
        scratch_shapes=[
            pltpu.VMEM((2, clusters), jnp.int32),
            pltpu.VMEM((1, clusters), jnp.int32),
            pltpu.SMEM((POOL,), jnp.int32),
            pltpu.SMEM(type_prec.shape, F32),
            pltpu.VMEM((POOL, K), F32),
            pltpu.VMEM((POOL, K), F32),
            pltpu.VMEM((OBS, POOL, members, K), BF),
            pltpu.VMEM((2 * POOL, K), F32),
            pltpu.VMEM((8, clusters), jnp.int32),
            pltpu.VMEM((OBS, 2 * POOL, K), F32),
            pltpu.VMEM((OBS, 8, clusters), jnp.int32),
            pltpu.SMEM((OBS, 8, clusters), jnp.int32),
            pltpu.VMEM((OBS * SLOTS, members, members), F32),
            pltpu.VMEM((OBS, POOL + 8, members), F32),
            pltpu.VMEM((OWN // UNIT, PACKED, members), BF),
            pltpu.VMEM((RELAYED, PER, members, K), BF),
            dma((6,)), dma,
            dma((2, 2, CORES)), dma((2, OBS)),
            dma((OBS, CHUNKS)), dma((OBS, CHUNKS)), dma((OBS, CHUNKS)),
            dma((2, RELAYED)), dma((RELAYED,)),
            dma((GROUPS,)),
            dma((3, GROUPS, UNITS)), dma((OBS, GROUPS, UNITS)),
            dma((CORES, GROUPS)), dma((OBS, 2, GROUPS)),
        ],
        compiler_params=pltpu.CompilerParams(
            collective_id=0, has_side_effects=True, vmem_limit_bytes=60 << 20
        ),
        name="solve",
    )(block_list.T, block_count.T, block_type, type_prec, obs_weight, innov, obs_pert)
    return pl.pallas_call(
        functools.partial(apply_kernel, clusters),
        out_shape=jax.ShapeDtypeStruct(state_pert.shape, BF),
        in_specs=[hbm] * 4,
        out_specs=hbm,
        scratch_shapes=[
            pltpu.SMEM(obs_clusters.shape, jnp.int32),
            pltpu.VMEM(packed.shape, BF), pltpu.VMEM(state_pert.shape, BF),
            pltpu.VMEM(state_mean.shape, F32), pltpu.VMEM(state_pert.shape, BF),
            dma((2, clusters // APPLY + 1)), dma((clusters // APPLY,)),
        ],
        compiler_params=pltpu.CompilerParams(vmem_limit_bytes=58 << 20),
        name="apply",
    )(obs_clusters, packed, state_pert, state_mean)


def solution(mesh):
    placed = (
        P("region", None, "obs"),
        P("region", "obs"),
        P(("region", "obs"), None, None),
        P(("region", "obs"), None),
        P(("region", "obs"), None),
        P(("region", "obs")),
        P(),
        P("region", "obs"),
        P("region", "obs"),
        P(),
    )
    return jax.shard_map(
        local, mesh=mesh, in_specs=placed, out_specs=P("region", None, "obs"), check_vma=False
    )
```

```python
import functools

import jax
import jax.numpy as jnp
from jax import lax
from jax.experimental import pallas as pl
from jax.experimental.pallas import tpu as pltpu
from jax.sharding import PartitionSpec as P

MESH = pl.DeviceIdType.MESH
BF = jnp.bfloat16
F32 = jnp.float32
K = 128
OBS = 4
CORES = 2
POOL = 32
SLOTS = POOL + 1
CHUNKS = 4
PER = POOL // CHUNKS
RELAYED = 1
DIRECT = CHUNKS - RELAYED
GROUP = 8
OWN = 32
GROUPS = OWN // GROUP
UNIT = 4
UNITS = GROUP // UNIT
PACKED = UNIT // 2 * K + 16


def split(a):
    high = a.astype(BF)
    return high, (a - high.astype(F32)).astype(BF)


def product(left, right):
    left_high, left_low = left
    right_high, right_low = right
    row = jnp.concatenate([right_high, right_low], axis=1)
    both = jnp.dot(
        jnp.concatenate([left_high, left_low], axis=1),
        jnp.concatenate([row, row], axis=0),
        preferred_element_type=F32,
    )
    return both[:, :K] + both[:, K:]


def root_stages(matrix, eye, result):
    w, w_parts = matrix, split(matrix)
    y, z = w_parts, None
    for step in range(6):
        if step:
            w = product(z, y)
            yield
            w_parts = split(w)
        inner = (product(w_parts, w_parts) - 4.5 * w) + 3.375 * eye
        yield
        inner = split(inner)
        turn = (1 / 16) * product(inner, inner) + ((24.609375 / 16) * eye - (8.625 / 16) * w)
        yield
        turn = split(turn)
        if step < 5:
            y = split(product(y, turn))
        if step:
            full = product(turn, z)
            z = split(full)
        else:
            z = turn
        yield
    result.append(full)


def inverse_root(matrices, eye):
    results = [[] for _ in matrices]
    live = [root_stages(matrix, eye, result) for matrix, result in zip(matrices, results)]
    for ahead in live[::2]:
        next(ahead)
    while live:
        live = [stages for stages in live if next(stages, True) is None]
    return [result[0] for result in results]


def places():
    rows = lax.broadcasted_iota(jnp.int32, (K, K), 0)
    columns = lax.broadcasted_iota(jnp.int32, (K, K), 1)
    return rows, columns


def solve_kernel(
    list_ref, count_ref, type_ref, prec_ref, weight_ref, innov_ref, pool_ref, out_ref,
    in_list, in_count, in_type, in_prec, in_weight, in_innov,
    pool, own_rows, own_lists, rows, lists, index, gram, proj, mine, stop,
    in_sem, local_sem, small_send, small_recv, send, twin_send, recv, r_send, r_recv,
    t_local, t_send, t_recv, f_send, f_recv,
):
    at, region = lax.axis_index("obs"), lax.axis_index("region")
    core = lax.rem(region, CORES)
    base = region - core
    twin = base + 1 - core
    odd = lax.rem(region // CORES, 2)
    beside = region + CORES * (1 - 2 * odd)
    me = lax.rem(at + odd, OBS)
    partner, cross, far = me + 1 - 2 * lax.rem(me, 2), 3 - me, lax.rem(me + 2, OBS)
    tile = me // 2
    primary = core == tile
    solver = lax.rem(me, 2) * CORES + core

    me_beside = lax.rem(at + 1 - odd, OBS)
    relay = core == me_beside // 2
    partner_beside = me_beside + 1 - 2 * lax.rem(me_beside, 2)

    def place(number):
        return lax.rem(number - odd + OBS, OBS)

    def remote(src, dst, send_sem, recv_sem, to_region, to):
        return pltpu.make_async_remote_copy(
            src_ref=src, dst_ref=dst, send_sem=send_sem, recv_sem=recv_sem,
            device_id={"region": to_region, "obs": place(to)}, device_id_type=MESH,
        )

    barrier = pltpu.get_barrier_semaphore()
    for other in range(1, OBS):
        for c in range(CORES):
            pl.semaphore_signal(
                barrier, inc=1, device_id={"region": base + c, "obs": lax.rem(at + other, OBS)}, device_id_type=MESH
            )
    pl.semaphore_signal(barrier, inc=1, device_id={"region": twin, "obs": at}, device_id_type=MESH)
    for to in (me, partner, cross):
        pl.semaphore_signal(barrier, inc=1, device_id={"region": beside, "obs": place(to)}, device_id_type=MESH)

    reads = []
    for j, (src, dst) in enumerate((
        (type_ref, in_type), (prec_ref, in_prec), (weight_ref, in_weight),
        (innov_ref, in_innov), (list_ref, in_list), (count_ref, in_count),
    )):
        reads.append(pltpu.make_async_copy(src, dst, in_sem.at[j]))
        reads[-1].start()
    for c in reads:
        c.wait()

    @pl.when(primary)
    def _():
        pltpu.make_async_copy(pool_ref, pool.at[me], local_sem).start()

    for b in range(POOL):
        weighted = in_weight[pl.ds(b, 1), :] * in_prec[in_type[b]]
        own_rows[pl.ds(b, 1), :] = weighted.astype(BF).astype(F32)
        own_rows[pl.ds(POOL + b, 1), :] = (weighted * in_innov[pl.ds(b, 1), :]).astype(BF).astype(F32)
    entry = lax.broadcasted_iota(jnp.int32, (2, K), 0)
    own_lists[...] = jnp.full((8, K), POOL, jnp.int32)
    own_lists[pl.ds(0, 2), :] = jnp.where(entry < in_count[...], in_list[...], POOL)
    place_row, place_column = places()
    eye = (place_row == place_column).astype(F32)
    for o in range(OBS):
        gram[o * SLOTS + POOL] = jnp.zeros((K, K), F32)
        proj[o, pl.ds(POOL, 8), :] = jnp.zeros((8, K), F32)
    pl.semaphore_wait(barrier, 10)

    def small(j, a, c):
        src, dst = ((own_rows, rows), (own_lists, lists))[j]
        return remote(src, dst.at[me], small_send.at[j, a, c], small_recv.at[j, me], base + c, 2 * core + a)

    def elsewhere(a, c):
        return jnp.logical_not(jnp.logical_and(primary, jnp.logical_and(2 * core + a == me, core == c)))

    for a in range(2):
        for c in range(CORES):
            @pl.when(elsewhere(a, c))
            def _():
                for j in range(2):
                    small(j, a, c).start()

    def piece(o, k):
        return pool.at[o, pl.ds(k * PER, PER)]

    def to_chip(src, o, k, to):
        return remote(src, piece(o, k), send.at[o, k], recv.at[o, k], region, to)

    def to_twin(src, o, k):
        return remote(src, piece(o, k), twin_send.at[o, k], recv.at[o, k], twin, me)

    def own_piece(k):
        return pool_ref.at[pl.ds(k * PER, PER)]

    def relay_out(k):
        return remote(own_piece(DIRECT + k), stop.at[k], r_send.at[0, k], r_recv.at[k], beside, partner)

    def relay_back(k):
        block = piece(partner_beside, DIRECT + k)
        return remote(stop.at[k], block, r_send.at[1, k], recv.at[partner_beside, DIRECT + k], beside, me)

    @pl.when(primary)
    def _():
        for k in range(RELAYED):
            relay_out(k).start()

        def body(k, _):
            @pl.when(k < DIRECT)
            def _():
                to_chip(own_piece(k), me, k, partner).start()

            to_twin(own_piece(k), me, k).start()
            return 0

        lax.fori_loop(0, CHUNKS, body, 0)
        rows[me] = own_rows[...]
        lists[me] = own_lists[...]

    @pl.when(jnp.logical_not(primary))
    def _():
        def body(k, _):
            to_chip(own_piece(k), me, k, cross).start()
            return 0

        lax.fori_loop(0, CHUNKS, body, 0)

    def arrived(o, k):
        to_twin(piece(o, k), o, k).wait_recv()

    def block_grams(o, k):
        for j in range(PER):
            b = k * PER + j
            pert = pool[o, b]
            weight = rows[o, pl.ds(b, 1), :]
            innov = rows[o, pl.ds(POOL + b, 1), :]
            scaled = (pert.astype(F32) * weight).astype(BF)
            lhs = jnp.concatenate([scaled, jnp.broadcast_to(innov, (16, K)).astype(BF)], axis=0)
            res = lax.dot_general(lhs, pert, (((1,), (1,)), ((), ())), preferred_element_type=F32)
            gram[o * SLOTS + b] = res[:K]
            proj[o, pl.ds(b, 1), :] = res[K:K + 1]

    def hand_on(k):
        first = isinstance(k, int)
        if not first or 1 <= k <= RELAYED:
            @pl.when(jnp.logical_and(relay, jnp.logical_and(k >= 1, k <= RELAYED)))
            def _():
                relay_out(k - 1).wait_recv()
                relay_back(k - 1).start()

        @pl.when(k < CHUNKS)
        def _():
            arrived(cross, k)

            @pl.when(primary)
            def _():
                to_chip(piece(cross, k), cross, k, partner).start()
                to_twin(piece(cross, k), cross, k).start()

            arrived(partner, k)

            @pl.when(primary)
            def _():
                to_twin(piece(partner, k), partner, k).start()

        if first:
            return

        @pl.when(k >= 2)
        def _():
            arrived(far, k - 2)

            @pl.when(primary)
            def _():
                to_twin(piece(far, k - 2), far, k - 2).start()

    hand_on(0)
    hand_on(1)
    for o in range(OBS):
        @pl.when(jnp.logical_not(jnp.logical_and(primary, me == o)))
        def _():
            for j, (src, dst) in enumerate(((own_rows, rows), (own_lists, lists))):
                remote(src, dst.at[o], small_send.at[j, 0, 0], small_recv.at[j, o], twin, me).wait_recv()
    to_index = pltpu.make_async_copy(lists, index, in_sem.at[0])
    to_index.start()

    @pl.when(primary)
    def _():
        pltpu.make_async_copy(pool_ref, pool.at[me], local_sem).wait()

    def grams(k):
        @pl.when(jnp.logical_not(primary))
        def _():
            arrived(me, k - 2)

        for o in (me, cross, partner):
            block_grams(o, k - 2)

        @pl.when(k >= 3)
        def _():
            block_grams(far, k - 3)

    def step(k, _):
        hand_on(k)
        grams(k)
        return 0

    def last_step(k, _):
        grams(k)
        hand_on(k)
        return 0

    lax.fori_loop(2, CHUNKS, step, 0)
    lax.fori_loop(CHUNKS, CHUNKS + 2, last_step, 0)
    block_grams(far, CHUNKS - 1)
    to_index.wait()

    def slot(of, g, unit, size):
        return out_ref.at[pl.ds(of * (OWN // UNIT) + g * UNITS + unit, size)]

    def unit_of(g, unit, size):
        return mine.at[pl.ds(g * UNITS + unit, size)]

    def t_first(j, of, g, unit, to):
        return remote(
            unit_of(g, unit, 1), slot(of, g, unit, 1), t_send.at[j, g, unit], t_recv.at[of, g, unit], base + tile, to
        )

    def t_keep(g):
        return pltpu.make_async_copy(unit_of(g, 0, UNITS), slot(solver, g, 0, UNITS), t_local.at[g])

    primary_int = primary.astype(jnp.int32)
    heard = primary_int * partner + (1 - primary_int) * cross
    onward = primary_int * cross + (1 - primary_int) * partner
    part = 1 - primary_int

    def t_pass(of, h, g, c, to):
        half = slot(of, g, h, 1)
        return remote(half, half, f_send.at[c, g], f_recv.at[of, h, g], region, to)

    def forward(g):
        for c in range(CORES):
            of = lax.rem(heard, 2) * CORES + c
            t_first(0, of, g, part, heard).wait_recv()
            t_pass(of, part, g, c, onward).start()

    upper = place_column >= place_row

    def solve_group(g, _):
        matrices, norms, vectors = [], [], []
        for i in range(GROUP):
            c = solver * OWN + g * GROUP + i
            total, vector = None, None
            for o in range(OBS):
                for m in range(2):
                    b = index[o, m, c]
                    one, row = gram[o * SLOTS + b], proj[o, pl.ds(b, 1), :]
                    total = one if total is None else total + one
                    vector = row if vector is None else vector + row
            matrix = eye + total * (1.0 / 127.0)
            square = jnp.sum(jnp.sum(matrix * matrix, axis=0, keepdims=True), axis=1, keepdims=True)
            scale = lax.rsqrt(square)
            matrices.append(matrix * scale)
            norms.append(scale)
            vectors.append(vector)
        full = inverse_root(matrices, eye)
        for u in range(UNITS):
            extra = []
            for q in range(UNIT // 2):
                roots, means = [], []
                for i in (u * UNIT + 2 * q, u * UNIT + 2 * q + 1):
                    row = vectors[i] * (norms[i] * (1.0 / 127.0))
                    column = jnp.sum(full[i] * row, axis=1, keepdims=True)
                    row = jnp.sum(full[i] * column, axis=0, keepdims=True)
                    roots.append(full[i] * jnp.sqrt(norms[i]))
                    means += split(row)
                extra += [jnp.sum(roots[1] * eye, axis=0, keepdims=True).astype(BF)] + means
                mine[g * UNITS + u, pl.ds(q * K, K), :] = jnp.where(upper, roots[0], roots[1]).astype(BF)
            extra.append(jnp.zeros((16 - len(extra), K), BF))
            mine[g * UNITS + u, pl.ds(UNIT // 2 * K, 16), :] = jnp.concatenate(extra, axis=0)
        for j, unit, to in ((0, 0, partner), (1, 1, cross), (0, 1, partner), (1, 0, cross)):
            t_first(j, solver, g, unit, to).start()

        @pl.when(primary)
        def _():
            t_keep(g).start()

        @pl.when(jnp.logical_not(primary))
        def _():
            for unit in range(UNITS):
                t_first(2, solver, g, unit, me).start()

        @pl.when(g > 0)
        def _():
            forward(g - 1)

        return 0

    lax.fori_loop(0, GROUPS, solve_group, 0)
    forward(GROUPS - 1)

    @pl.when(primary)
    def _():
        for g in range(GROUPS):
            for unit in range(UNITS):
                t_first(2, lax.rem(me, 2) * CORES + 1 - core, g, unit, me).wait_recv()
            t_keep(g).wait()

        for k in range(DIRECT):
            to_chip(own_piece(k), me, k, partner).wait_send()
        for k in range(RELAYED):
            relay_out(k).wait_send()
        for k in range(CHUNKS):
            to_chip(piece(cross, k), cross, k, partner).wait_send()
            to_twin(own_piece(k), me, k).wait_send()
            for o in (cross, partner, far):
                to_twin(piece(o, k), o, k).wait_send()

    @pl.when(jnp.logical_not(primary))
    def _():
        for g in range(GROUPS):
            for c in range(CORES):
                of = lax.rem(far, 2) * CORES + c
                for h in range(2):
                    t_pass(of, h, g, c, onward).wait_recv()
            for unit in range(UNITS):
                t_first(2, solver, g, unit, me).wait_send()

        for k in range(CHUNKS):
            to_chip(own_piece(k), me, k, cross).wait_send()

    for g in range(GROUPS):
        for unit in range(UNITS):
            t_first(0, solver, g, unit, partner).wait_send()
            t_first(1, solver, g, unit, cross).wait_send()
        for c in range(CORES):
            of = lax.rem(heard, 2) * CORES + c
            t_first(0, of, g, 1 - part, heard).wait_recv()
            t_pass(of, part, g, c, onward).wait_send()
    @pl.when(relay)
    def _():
        for k in range(RELAYED):
            relay_back(k).wait_send()

    for a in range(2):
        for c in range(CORES):
            @pl.when(elsewhere(a, c))
            def _():
                for j in range(2):
                    small(j, a, c).wait_send()


APPLY = 32


def apply_kernel(clusters, count_ref, packed_ref, x_ref, mean_ref, out_ref, counts, packed_in, x_in, mean, result, in_sem, out_sem):
    steps = clusters // APPLY

    def reads(s):
        here, units = pl.ds(s * APPLY, APPLY), pl.ds(s * (APPLY // UNIT), APPLY // UNIT)
        return (
            pltpu.make_async_copy(packed_ref.at[units], packed_in.at[units], in_sem.at[0, s]),
            pltpu.make_async_copy(x_ref.at[here], x_in.at[here], in_sem.at[1, s]),
        )

    def write(s):
        here = pl.ds(s * APPLY, APPLY)
        return pltpu.make_async_copy(result.at[here], out_ref.at[here], out_sem.at[s])

    small = (
        pltpu.make_async_copy(count_ref, counts, in_sem.at[0, steps]),
        pltpu.make_async_copy(mean_ref, mean, in_sem.at[1, steps]),
    )
    for c in reads(0) + small:
        c.start()
    for s in range(1, steps):
        for c in reads(s):
            c.start()
    place_row, place_column = places()
    diagonal, upper, lower = place_row == place_column, place_column >= place_row, place_column < place_row

    eye = diagonal.astype(BF)
    for c in small:
        c.wait()
    count = counts[lax.axis_index("region")]

    def body(s, _):
        for c in reads(s):
            c.wait()
        for u in range(APPLY // UNIT):
            unit = s * (APPLY // UNIT) + u
            extra = packed_in[unit, pl.ds(UNIT // 2 * K, 16), :].astype(F32)
            for q in range(UNIT // 2):
                packed = packed_in[unit, pl.ds(q * K, K), :]
                straight = packed.astype(F32)
                turned = straight.T
                roots = (
                    jnp.where(upper, straight, turned),
                    jnp.where(lower, straight, jnp.where(diagonal, extra[5 * q:5 * q + 1], turned)),
                )
                for i in range(2):
                    c = unit * UNIT + 2 * q + i
                    m = 5 * q + 1 + 2 * i
                    solved = (roots[i] + (extra[m:m + 1] + extra[m + 1:m + 2])).astype(BF)
                    solved = jnp.where(c < count, solved, eye)
                    mixed = jnp.dot(solved, x_in[c], preferred_element_type=F32)
                    result[c] = (mixed + mean[pl.ds(c, 1), :]).astype(BF)
        write(s).start()
        return 0

    lax.fori_loop(0, steps, body, 0)
    for s in range(steps):
        write(s).wait()


def local(
    state_pert, state_mean, obs_pert, innov, obs_weight, block_type, type_prec, block_list, block_count, obs_clusters
):
    clusters, members, points = state_pert.shape
    dma = pltpu.SemaphoreType.DMA
    hbm, anywhere = pl.BlockSpec(memory_space=pltpu.HBM), pl.BlockSpec(memory_space=pl.ANY)
    packed = pl.pallas_call(
        solve_kernel,
        out_shape=jax.ShapeDtypeStruct((clusters // UNIT, PACKED, members), BF),
        in_specs=[hbm] * 7,
        out_specs=anywhere,
        scratch_shapes=[
            pltpu.VMEM((2, clusters), jnp.int32),
            pltpu.VMEM((1, clusters), jnp.int32),
            pltpu.SMEM((POOL,), jnp.int32),
            pltpu.SMEM(type_prec.shape, F32),
            pltpu.VMEM((POOL, K), F32),
            pltpu.VMEM((POOL, K), F32),
            pltpu.VMEM((OBS, POOL, members, K), BF),
            pltpu.VMEM((2 * POOL, K), F32),
            pltpu.VMEM((8, clusters), jnp.int32),
            pltpu.VMEM((OBS, 2 * POOL, K), F32),
            pltpu.VMEM((OBS, 8, clusters), jnp.int32),
            pltpu.SMEM((OBS, 8, clusters), jnp.int32),
            pltpu.VMEM((OBS * SLOTS, members, members), F32),
            pltpu.VMEM((OBS, POOL + 8, members), F32),
            pltpu.VMEM((OWN // UNIT, PACKED, members), BF),
            pltpu.VMEM((RELAYED, PER, members, K), BF),
            dma((6,)), dma,
            dma((2, 2, CORES)), dma((2, OBS)),
            dma((OBS, CHUNKS)), dma((OBS, CHUNKS)), dma((OBS, CHUNKS)),
            dma((2, RELAYED)), dma((RELAYED,)),
            dma((GROUPS,)),
            dma((3, GROUPS, UNITS)), dma((OBS, GROUPS, UNITS)),
            dma((CORES, GROUPS)), dma((OBS, 2, GROUPS)),
        ],
        compiler_params=pltpu.CompilerParams(
            collective_id=0, has_side_effects=True, vmem_limit_bytes=60 << 20
        ),
        name="solve",
    )(block_list.T, block_count.T, block_type, type_prec, obs_weight, innov, obs_pert)
    return pl.pallas_call(
        functools.partial(apply_kernel, clusters),
        out_shape=jax.ShapeDtypeStruct(state_pert.shape, BF),
        in_specs=[hbm] * 4,
        out_specs=hbm,
        scratch_shapes=[
            pltpu.SMEM(obs_clusters.shape, jnp.int32),
            pltpu.VMEM(packed.shape, BF), pltpu.VMEM(state_pert.shape, BF),
            pltpu.VMEM(state_mean.shape, F32), pltpu.VMEM(state_pert.shape, BF),
            dma((2, clusters // APPLY + 1)), dma((clusters // APPLY,)),
        ],
        compiler_params=pltpu.CompilerParams(vmem_limit_bytes=58 << 20),
        name="apply",
    )(obs_clusters, packed, state_pert, state_mean)


def solution(mesh):
    placed = (
        P("region", None, "obs"),
        P("region", "obs"),
        P(("region", "obs"), None, None),
        P(("region", "obs"), None),
        P(("region", "obs"), None),
        P(("region", "obs")),
        P(),
        P("region", "obs"),
        P("region", "obs"),
        P(),
    )
    return jax.shard_map(
        local, mesh=mesh, in_specs=placed, out_specs=P("region", None, "obs"), check_vma=False
    )
```

```python
import functools

import jax
import jax.numpy as jnp
from jax import lax
from jax.experimental import pallas as pl
from jax.experimental.pallas import tpu as pltpu
from jax.sharding import PartitionSpec as P

MESH = pl.DeviceIdType.MESH
BF = jnp.bfloat16
F32 = jnp.float32
K = 128
OBS = 4
CORES = 2
POOL = 32
SLOTS = POOL + 1
CHUNKS = 4
PER = POOL // CHUNKS
RELAYED = 1
DIRECT = CHUNKS - RELAYED
GROUP = 8
OWN = 32
GROUPS = OWN // GROUP
UNIT = 4
UNITS = GROUP // UNIT
PACKED = UNIT // 2 * K + 16


def split(a):
    high = a.astype(BF)
    return high, (a - high.astype(F32)).astype(BF)


def product(left, right):
    left_high, left_low = left
    right_high, right_low = right
    row = jnp.concatenate([right_high, right_low], axis=1)
    both = jnp.dot(
        jnp.concatenate([left_high, left_low], axis=1),
        jnp.concatenate([row, row], axis=0),
        preferred_element_type=F32,
    )
    return both[:, :K] + both[:, K:]


def root_stages(matrix, eye, result):
    w, w_parts = matrix, split(matrix)
    y, z = w_parts, None
    for step in range(6):
        if step:
            w = product(z, y)
            yield
            w_parts = split(w)
        inner = (product(w_parts, w_parts) - 4.5 * w) + 3.375 * eye
        yield
        inner = split(inner)
        turn = (1 / 16) * product(inner, inner) + ((24.609375 / 16) * eye - (8.625 / 16) * w)
        yield
        turn = split(turn)
        if step < 5:
            y = split(product(y, turn))
        if step:
            full = product(turn, z)
            z = split(full)
        else:
            z = turn
        yield
    result.append(full)


def inverse_root(matrices, eye):
    results = [[] for _ in matrices]
    live = [root_stages(matrix, eye, result) for matrix, result in zip(matrices, results)]
    for ahead in live[::2]:
        next(ahead)
    while live:
        live = [stages for stages in live if next(stages, True) is None]
    return [result[0] for result in results]


def places():
    rows = lax.broadcasted_iota(jnp.int32, (K, K), 0)
    columns = lax.broadcasted_iota(jnp.int32, (K, K), 1)
    return rows, columns


def solve_kernel(
    list_ref, count_ref, type_ref, prec_ref, weight_ref, innov_ref, pool_ref, out_ref,
    in_list, in_count, in_type, in_prec, in_weight, in_innov,
    pool, own_rows, own_lists, rows, lists, index, gram, proj, mine, stop,
    in_sem, local_sem, small_send, small_recv, send, twin_send, recv, r_send, r_recv,
    t_local, t_send, t_recv, f_send, f_recv,
):
    at, region = lax.axis_index("obs"), lax.axis_index("region")
    core = lax.rem(region, CORES)
    base = region - core
    twin = base + 1 - core
    odd = lax.rem(region // CORES, 2)
    beside = region + CORES * (1 - 2 * odd)
    me = lax.rem(at + odd, OBS)
    partner, cross, far = me + 1 - 2 * lax.rem(me, 2), 3 - me, lax.rem(me + 2, OBS)
    tile = me // 2
    primary = core == tile
    solver = lax.rem(me, 2) * CORES + core

    me_beside = lax.rem(at + 1 - odd, OBS)
    relay = core == me_beside // 2
    partner_beside = me_beside + 1 - 2 * lax.rem(me_beside, 2)

    def place(number):
        return lax.rem(number - odd + OBS, OBS)

    def remote(src, dst, send_sem, recv_sem, to_region, to):
        return pltpu.make_async_remote_copy(
            src_ref=src, dst_ref=dst, send_sem=send_sem, recv_sem=recv_sem,
            device_id={"region": to_region, "obs": place(to)}, device_id_type=MESH,
        )

    barrier = pltpu.get_barrier_semaphore()
    for other in range(1, OBS):
        for c in range(CORES):
            pl.semaphore_signal(
                barrier, inc=1, device_id={"region": base + c, "obs": lax.rem(at + other, OBS)}, device_id_type=MESH
            )
    pl.semaphore_signal(barrier, inc=1, device_id={"region": twin, "obs": at}, device_id_type=MESH)
    for to in (me, partner, cross):
        pl.semaphore_signal(barrier, inc=1, device_id={"region": beside, "obs": place(to)}, device_id_type=MESH)

    reads = []
    for j, (src, dst) in enumerate((
        (type_ref, in_type), (prec_ref, in_prec), (weight_ref, in_weight),
        (innov_ref, in_innov), (list_ref, in_list), (count_ref, in_count),
    )):
        reads.append(pltpu.make_async_copy(src, dst, in_sem.at[j]))
        reads[-1].start()
    for c in reads:
        c.wait()

    @pl.when(primary)
    def _():
        pltpu.make_async_copy(pool_ref, pool.at[me], local_sem).start()

    for b in range(POOL):
        weighted = in_weight[pl.ds(b, 1), :] * in_prec[in_type[b]]
        own_rows[pl.ds(b, 1), :] = weighted.astype(BF).astype(F32)
        own_rows[pl.ds(POOL + b, 1), :] = (weighted * in_innov[pl.ds(b, 1), :]).astype(BF).astype(F32)
    entry = lax.broadcasted_iota(jnp.int32, (2, K), 0)
    own_lists[...] = jnp.full((8, K), POOL, jnp.int32)
    own_lists[pl.ds(0, 2), :] = jnp.where(entry < in_count[...], in_list[...], POOL)
    place_row, place_column = places()
    eye = (place_row == place_column).astype(F32)
    for o in range(OBS):
        gram[o * SLOTS + POOL] = jnp.zeros((K, K), F32)
        proj[o, pl.ds(POOL, 8), :] = jnp.zeros((8, K), F32)
    pl.semaphore_wait(barrier, 10)

    def small(j, a, c):
        src, dst = ((own_rows, rows), (own_lists, lists))[j]
        return remote(src, dst.at[me], small_send.at[j, a, c], small_recv.at[j, me], base + c, 2 * core + a)

    def elsewhere(a, c):
        return jnp.logical_not(jnp.logical_and(primary, jnp.logical_and(2 * core + a == me, core == c)))

    for a in range(2):
        for c in range(CORES):
            @pl.when(elsewhere(a, c))
            def _():
                for j in range(2):
                    small(j, a, c).start()

    def piece(o, k):
        return pool.at[o, pl.ds(k * PER, PER)]

    def to_chip(src, o, k, to):
        return remote(src, piece(o, k), send.at[o, k], recv.at[o, k], region, to)

    def to_twin(src, o, k):
        return remote(src, piece(o, k), twin_send.at[o, k], recv.at[o, k], twin, me)

    def own_piece(k):
        return pool_ref.at[pl.ds(k * PER, PER)]

    def relay_out(k):
        return remote(own_piece(DIRECT + k), stop.at[k], r_send.at[0, k], r_recv.at[k], beside, partner)

    def relay_back(k):
        block = piece(partner_beside, DIRECT + k)
        return remote(stop.at[k], block, r_send.at[1, k], recv.at[partner_beside, DIRECT + k], beside, me)

    @pl.when(primary)
    def _():
        for k in range(RELAYED):
            relay_out(k).start()

        def body(k, _):
            @pl.when(k < DIRECT)
            def _():
                to_chip(own_piece(k), me, k, partner).start()

            to_twin(own_piece(k), me, k).start()
            return 0

        lax.fori_loop(0, CHUNKS, body, 0)
        rows[me] = own_rows[...]
        lists[me] = own_lists[...]

    @pl.when(jnp.logical_not(primary))
    def _():
        def body(k, _):
            to_chip(own_piece(k), me, k, cross).start()
            return 0

        lax.fori_loop(0, CHUNKS, body, 0)

    def arrived(o, k):
        to_twin(piece(o, k), o, k).wait_recv()

    def block_grams(o, k):
        for j in range(PER):
            b = k * PER + j
            pert = pool[o, b]
            weight = rows[o, pl.ds(b, 1), :]
            innov = rows[o, pl.ds(POOL + b, 1), :]
            scaled = (pert.astype(F32) * weight).astype(BF)
            lhs = jnp.concatenate([scaled, jnp.broadcast_to(innov, (16, K)).astype(BF)], axis=0)
            res = lax.dot_general(lhs, pert, (((1,), (1,)), ((), ())), preferred_element_type=F32)
            gram[o * SLOTS + b] = res[:K]
            proj[o, pl.ds(b, 1), :] = res[K:K + 1]

    def hand_on(k):
        first = isinstance(k, int)
        if not first or 1 <= k <= RELAYED:
            @pl.when(jnp.logical_and(relay, jnp.logical_and(k >= 1, k <= RELAYED)))
            def _():
                relay_out(k - 1).wait_recv()
                relay_back(k - 1).start()

        @pl.when(k < CHUNKS)
        def _():
            arrived(cross, k)

            @pl.when(primary)
            def _():
                to_chip(piece(cross, k), cross, k, partner).start()
                to_twin(piece(cross, k), cross, k).start()

            arrived(partner, k)

            @pl.when(primary)
            def _():
                to_twin(piece(partner, k), partner, k).start()

        if first:
            return

        @pl.when(k >= 2)
        def _():
            arrived(far, k - 2)

            @pl.when(primary)
            def _():
                to_twin(piece(far, k - 2), far, k - 2).start()

    hand_on(0)
    hand_on(1)
    for o in range(OBS):
        @pl.when(jnp.logical_not(jnp.logical_and(primary, me == o)))
        def _():
            for j, (src, dst) in enumerate(((own_rows, rows), (own_lists, lists))):
                remote(src, dst.at[o], small_send.at[j, 0, 0], small_recv.at[j, o], twin, me).wait_recv()
    to_index = pltpu.make_async_copy(lists, index, in_sem.at[0])
    to_index.start()

    @pl.when(primary)
    def _():
        pltpu.make_async_copy(pool_ref, pool.at[me], local_sem).wait()

    def grams(k):
        @pl.when(jnp.logical_not(primary))
        def _():
            arrived(me, k - 2)

        for o in (me, cross, partner):
            block_grams(o, k - 2)

        @pl.when(k >= 3)
        def _():
            block_grams(far, k - 3)

    def step(k, _):
        hand_on(k)
        grams(k)
        return 0

    def last_step(k, _):
        grams(k)
        hand_on(k)
        return 0

    lax.fori_loop(2, CHUNKS, step, 0)
    lax.fori_loop(CHUNKS, CHUNKS + 2, last_step, 0)
    block_grams(far, CHUNKS - 1)
    to_index.wait()

    def slot(of, g, unit, size):
        return out_ref.at[pl.ds(of * (OWN // UNIT) + g * UNITS + unit, size)]

    def unit_of(g, unit, size):
        return mine.at[pl.ds(g * UNITS + unit, size)]

    def t_first(j, of, g, unit, to):
        return remote(
            unit_of(g, unit, 1), slot(of, g, unit, 1), t_send.at[j, g, unit], t_recv.at[of, g, unit], base + tile, to
        )

    def t_keep(g):
        return pltpu.make_async_copy(unit_of(g, 0, UNITS), slot(solver, g, 0, UNITS), t_local.at[g])

    primary_int = primary.astype(jnp.int32)
    heard = primary_int * partner + (1 - primary_int) * cross
    onward = primary_int * cross + (1 - primary_int) * partner
    part = 1 - primary_int

    def t_pass(of, h, g, c, to):
        half = slot(of, g, h, 1)
        return remote(half, half, f_send.at[c, g], f_recv.at[of, h, g], region, to)

    def forward(g):
        for c in range(CORES):
            of = lax.rem(heard, 2) * CORES + c
            t_first(0, of, g, part, heard).wait_recv()
            t_pass(of, part, g, c, onward).start()

    upper = place_column >= place_row

    def solve_group(g, _):
        matrices, norms, vectors = [], [], []
        for i in range(GROUP):
            c = solver * OWN + g * GROUP + i
            total, vector = None, None
            for o in range(OBS):
                for m in range(2):
                    b = index[o, m, c]
                    one, row = gram[o * SLOTS + b], proj[o, pl.ds(b, 1), :]
                    total = one if total is None else total + one
                    vector = row if vector is None else vector + row
            matrix = eye + total * (1.0 / 127.0)
            square = jnp.sum(jnp.sum(matrix * matrix, axis=0, keepdims=True), axis=1, keepdims=True)
            scale = lax.rsqrt(square)
            matrices.append(matrix * scale)
            norms.append(scale)
            vectors.append(vector)
        full = inverse_root(matrices, eye)
        for u in range(UNITS):
            extra = []
            for q in range(UNIT // 2):
                roots, means = [], []
                for i in (u * UNIT + 2 * q, u * UNIT + 2 * q + 1):
                    row = vectors[i] * (norms[i] * (1.0 / 127.0))
                    column = jnp.sum(full[i] * row, axis=1, keepdims=True)
                    row = jnp.sum(full[i] * column, axis=0, keepdims=True)
                    roots.append(full[i] * jnp.sqrt(norms[i]))
                    means += split(row)
                extra += [jnp.sum(roots[1] * eye, axis=0, keepdims=True).astype(BF)] + means
                mine[g * UNITS + u, pl.ds(q * K, K), :] = jnp.where(upper, roots[0], roots[1]).astype(BF)
            extra.append(jnp.zeros((16 - len(extra), K), BF))
            mine[g * UNITS + u, pl.ds(UNIT // 2 * K, 16), :] = jnp.concatenate(extra, axis=0)
        for j, unit, to in ((0, 0, partner), (1, 1, cross), (0, 1, partner), (1, 0, cross)):
            t_first(j, solver, g, unit, to).start()

        @pl.when(primary)
        def _():
            t_keep(g).start()

        @pl.when(jnp.logical_not(primary))
        def _():
            for unit in range(UNITS):
                t_first(2, solver, g, unit, me).start()

        @pl.when(g > 0)
        def _():
            forward(g - 1)

        return 0

    lax.fori_loop(0, GROUPS, solve_group, 0)
    forward(GROUPS - 1)

    @pl.when(primary)
    def _():
        for g in range(GROUPS):
            for unit in range(UNITS):
                t_first(2, lax.rem(me, 2) * CORES + 1 - core, g, unit, me).wait_recv()
            t_keep(g).wait()

        for k in range(DIRECT):
            to_chip(own_piece(k), me, k, partner).wait_send()
        for k in range(RELAYED):
            relay_out(k).wait_send()
        for k in range(CHUNKS):
            to_chip(piece(cross, k), cross, k, partner).wait_send()
            to_twin(own_piece(k), me, k).wait_send()
            for o in (cross, partner, far):
                to_twin(piece(o, k), o, k).wait_send()

    @pl.when(jnp.logical_not(primary))
    def _():
        for g in range(GROUPS):
            for c in range(CORES):
                of = lax.rem(far, 2) * CORES + c
                for h in range(2):
                    t_pass(of, h, g, c, onward).wait_recv()
            for unit in range(UNITS):
                t_first(2, solver, g, unit, me).wait_send()

        for k in range(CHUNKS):
            to_chip(own_piece(k), me, k, cross).wait_send()

    for g in range(GROUPS):
        for unit in range(UNITS):
            t_first(0, solver, g, unit, partner).wait_send()
            t_first(1, solver, g, unit, cross).wait_send()
        for c in range(CORES):
            of = lax.rem(heard, 2) * CORES + c
            t_first(0, of, g, 1 - part, heard).wait_recv()
            t_pass(of, part, g, c, onward).wait_send()
    @pl.when(relay)
    def _():
        for k in range(RELAYED):
            relay_back(k).wait_send()

    for a in range(2):
        for c in range(CORES):
            @pl.when(elsewhere(a, c))
            def _():
                for j in range(2):
                    small(j, a, c).wait_send()


APPLY = 32


def apply_kernel(clusters, count_ref, packed_ref, x_ref, mean_ref, out_ref, counts, packed_in, x_in, mean, result, in_sem, out_sem):
    steps = clusters // APPLY

    def reads(s):
        here, units = pl.ds(s * APPLY, APPLY), pl.ds(s * (APPLY // UNIT), APPLY // UNIT)
        return (
            pltpu.make_async_copy(packed_ref.at[units], packed_in.at[units], in_sem.at[0, s]),
            pltpu.make_async_copy(x_ref.at[here], x_in.at[here], in_sem.at[1, s]),
        )

    def write(s, half):
        here = pl.ds(s * APPLY + half * (APPLY // 2), APPLY // 2)
        return pltpu.make_async_copy(result.at[here], out_ref.at[here], out_sem.at[half, s])

    small = (
        pltpu.make_async_copy(count_ref, counts, in_sem.at[0, steps]),
        pltpu.make_async_copy(mean_ref, mean, in_sem.at[1, steps]),
    )
    for c in reads(0) + small:
        c.start()
    for s in range(1, steps):
        for c in reads(s):
            c.start()
    place_row, place_column = places()
    diagonal, upper, lower = place_row == place_column, place_column >= place_row, place_column < place_row

    eye = diagonal.astype(BF)
    for c in small:
        c.wait()
    count = counts[lax.axis_index("region")]

    def body(s, _):
        for c in reads(s):
            c.wait()
        for u in range(APPLY // UNIT):
            unit = s * (APPLY // UNIT) + u
            extra = packed_in[unit, pl.ds(UNIT // 2 * K, 16), :].astype(F32)
            for q in range(UNIT // 2):
                packed = packed_in[unit, pl.ds(q * K, K), :]
                straight = packed.astype(F32)
                turned = straight.T
                roots = (
                    jnp.where(upper, straight, turned),
                    jnp.where(lower, straight, jnp.where(diagonal, extra[5 * q:5 * q + 1], turned)),
                )
                for i in range(2):
                    c = unit * UNIT + 2 * q + i
                    m = 5 * q + 1 + 2 * i
                    solved = (roots[i] + (extra[m:m + 1] + extra[m + 1:m + 2])).astype(BF)
                    solved = jnp.where(c < count, solved, eye)
                    mixed = jnp.dot(solved, x_in[c], preferred_element_type=F32)
                    result[c] = (mixed + mean[pl.ds(c, 1), :]).astype(BF)
            if u == APPLY // UNIT // 2 - 1:
                write(s, 0).start()
        write(s, 1).start()
        return 0

    lax.fori_loop(0, steps, body, 0)
    for s in range(steps):
        write(s, 0).wait()
        write(s, 1).wait()


def local(
    state_pert, state_mean, obs_pert, innov, obs_weight, block_type, type_prec, block_list, block_count, obs_clusters
):
    clusters, members, points = state_pert.shape
    dma = pltpu.SemaphoreType.DMA
    hbm, anywhere = pl.BlockSpec(memory_space=pltpu.HBM), pl.BlockSpec(memory_space=pl.ANY)
    packed = pl.pallas_call(
        solve_kernel,
        out_shape=jax.ShapeDtypeStruct((clusters // UNIT, PACKED, members), BF),
        in_specs=[hbm] * 7,
        out_specs=anywhere,
        scratch_shapes=[
            pltpu.VMEM((2, clusters), jnp.int32),
            pltpu.VMEM((1, clusters), jnp.int32),
            pltpu.SMEM((POOL,), jnp.int32),
            pltpu.SMEM(type_prec.shape, F32),
            pltpu.VMEM((POOL, K), F32),
            pltpu.VMEM((POOL, K), F32),
            pltpu.VMEM((OBS, POOL, members, K), BF),
            pltpu.VMEM((2 * POOL, K), F32),
            pltpu.VMEM((8, clusters), jnp.int32),
            pltpu.VMEM((OBS, 2 * POOL, K), F32),
            pltpu.VMEM((OBS, 8, clusters), jnp.int32),
            pltpu.SMEM((OBS, 8, clusters), jnp.int32),
            pltpu.VMEM((OBS * SLOTS, members, members), F32),
            pltpu.VMEM((OBS, POOL + 8, members), F32),
            pltpu.VMEM((OWN // UNIT, PACKED, members), BF),
            pltpu.VMEM((RELAYED, PER, members, K), BF),
            dma((6,)), dma,
            dma((2, 2, CORES)), dma((2, OBS)),
            dma((OBS, CHUNKS)), dma((OBS, CHUNKS)), dma((OBS, CHUNKS)),
            dma((2, RELAYED)), dma((RELAYED,)),
            dma((GROUPS,)),
            dma((3, GROUPS, UNITS)), dma((OBS, GROUPS, UNITS)),
            dma((CORES, GROUPS)), dma((OBS, 2, GROUPS)),
        ],
        compiler_params=pltpu.CompilerParams(
            collective_id=0, has_side_effects=True, vmem_limit_bytes=60 << 20
        ),
        name="solve",
    )(block_list.T, block_count.T, block_type, type_prec, obs_weight, innov, obs_pert)
    return pl.pallas_call(
        functools.partial(apply_kernel, clusters),
        out_shape=jax.ShapeDtypeStruct(state_pert.shape, BF),
        in_specs=[hbm] * 4,
        out_specs=hbm,
        scratch_shapes=[
            pltpu.SMEM(obs_clusters.shape, jnp.int32),
            pltpu.VMEM(packed.shape, BF), pltpu.VMEM(state_pert.shape, BF),
            pltpu.VMEM(state_mean.shape, F32), pltpu.VMEM(state_pert.shape, BF),
            dma((2, clusters // APPLY + 1)), dma((2, clusters // APPLY)),
        ],
        compiler_params=pltpu.CompilerParams(vmem_limit_bytes=58 << 20),
        name="apply",
    )(obs_clusters, packed, state_pert, state_mean)


def solution(mesh):
    placed = (
        P("region", None, "obs"),
        P("region", "obs"),
        P(("region", "obs"), None, None),
        P(("region", "obs"), None),
        P(("region", "obs"), None),
        P(("region", "obs")),
        P(),
        P("region", "obs"),
        P("region", "obs"),
        P(),
    )
    return jax.shard_map(
        local, mesh=mesh, in_specs=placed, out_specs=P("region", None, "obs"), check_vma=False
    )
```

```python
import functools

import jax
import jax.numpy as jnp
from jax import lax
from jax.experimental import pallas as pl
from jax.experimental.pallas import tpu as pltpu
from jax.sharding import PartitionSpec as P

MESH = pl.DeviceIdType.MESH
BF = jnp.bfloat16
F32 = jnp.float32
K = 128
OBS = 4
CORES = 2
POOL = 32
SLOTS = POOL + 1
CHUNKS = 4
PER = POOL // CHUNKS
RELAYED = 1
DIRECT = CHUNKS - RELAYED
GROUP = 8
OWN = 32
GROUPS = OWN // GROUP
UNIT = 4
UNITS = GROUP // UNIT
PACKED = UNIT // 2 * K + 16


def split(a):
    high = a.astype(BF)
    return high, (a - high.astype(F32)).astype(BF)


def product(left, right):
    left_high, left_low = left
    right_high, right_low = right
    row = jnp.concatenate([right_high, right_low], axis=1)
    both = jnp.dot(
        jnp.concatenate([left_high, left_low], axis=1),
        jnp.concatenate([row, row], axis=0),
        preferred_element_type=F32,
    )
    return both[:, :K] + both[:, K:]


def root_stages(matrix, eye, result):
    w, w_parts = matrix, split(matrix)
    y, z = w_parts, None
    for step in range(6):
        if step:
            w = product(z, y)
            yield
            w_parts = split(w)
        inner = (product(w_parts, w_parts) - 4.5 * w) + 3.375 * eye
        yield
        inner = split(inner)
        turn = (1 / 16) * product(inner, inner) + ((24.609375 / 16) * eye - (8.625 / 16) * w)
        yield
        turn = split(turn)
        if step < 5:
            y = split(product(y, turn))
        if step:
            full = product(turn, z)
            z = split(full)
        else:
            z = turn
        yield
    result.append(full)


def inverse_root(matrices, eye):
    results = [[] for _ in matrices]
    live = [root_stages(matrix, eye, result) for matrix, result in zip(matrices, results)]
    for ahead in live[::2]:
        next(ahead)
    while live:
        live = [stages for stages in live if next(stages, True) is None]
    return [result[0] for result in results]


def places():
    rows = lax.broadcasted_iota(jnp.int32, (K, K), 0)
    columns = lax.broadcasted_iota(jnp.int32, (K, K), 1)
    return rows, columns


def solve_kernel(
    list_ref, count_ref, type_ref, prec_ref, weight_ref, innov_ref, pool_ref, out_ref,
    in_list, in_count, in_type, in_prec, in_weight, in_innov,
    pool, own_rows, own_lists, rows, lists, index, gram, proj, mine, stop,
    in_sem, local_sem, small_send, small_recv, send, twin_send, recv, r_send, r_recv,
    t_local, t_send, t_recv, f_send, f_recv,
):
    at, region = lax.axis_index("obs"), lax.axis_index("region")
    core = lax.rem(region, CORES)
    base = region - core
    twin = base + 1 - core
    odd = lax.rem(region // CORES, 2)
    beside = region + CORES * (1 - 2 * odd)
    me = lax.rem(at + odd, OBS)
    partner, cross, far = me + 1 - 2 * lax.rem(me, 2), 3 - me, lax.rem(me + 2, OBS)
    tile = me // 2
    primary = core == tile
    solver = lax.rem(me, 2) * CORES + core

    me_beside = lax.rem(at + 1 - odd, OBS)
    relay = core == me_beside // 2
    partner_beside = me_beside + 1 - 2 * lax.rem(me_beside, 2)

    def place(number):
        return lax.rem(number - odd + OBS, OBS)

    def remote(src, dst, send_sem, recv_sem, to_region, to):
        return pltpu.make_async_remote_copy(
            src_ref=src, dst_ref=dst, send_sem=send_sem, recv_sem=recv_sem,
            device_id={"region": to_region, "obs": place(to)}, device_id_type=MESH,
        )

    barrier = pltpu.get_barrier_semaphore()
    for other in range(1, OBS):
        for c in range(CORES):
            pl.semaphore_signal(
                barrier, inc=1, device_id={"region": base + c, "obs": lax.rem(at + other, OBS)}, device_id_type=MESH
            )
    pl.semaphore_signal(barrier, inc=1, device_id={"region": twin, "obs": at}, device_id_type=MESH)
    for to in (me, partner, cross):
        pl.semaphore_signal(barrier, inc=1, device_id={"region": beside, "obs": place(to)}, device_id_type=MESH)

    reads = []
    for j, (src, dst) in enumerate((
        (type_ref, in_type), (prec_ref, in_prec), (weight_ref, in_weight),
        (innov_ref, in_innov), (list_ref, in_list), (count_ref, in_count),
    )):
        reads.append(pltpu.make_async_copy(src, dst, in_sem.at[j]))
        reads[-1].start()
    for c in reads:
        c.wait()

    @pl.when(primary)
    def _():
        pltpu.make_async_copy(pool_ref, pool.at[me], local_sem).start()

    for b in range(POOL):
        weighted = in_weight[pl.ds(b, 1), :] * in_prec[in_type[b]]
        own_rows[pl.ds(b, 1), :] = weighted.astype(BF).astype(F32)
        own_rows[pl.ds(POOL + b, 1), :] = (weighted * in_innov[pl.ds(b, 1), :]).astype(BF).astype(F32)
    entry = lax.broadcasted_iota(jnp.int32, (2, K), 0)
    own_lists[...] = jnp.full((8, K), POOL, jnp.int32)
    own_lists[pl.ds(0, 2), :] = jnp.where(entry < in_count[...], in_list[...], POOL)
    place_row, place_column = places()
    eye = (place_row == place_column).astype(F32)
    for o in range(OBS):
        gram[o * SLOTS + POOL] = jnp.zeros((K, K), F32)
        proj[o, pl.ds(POOL, 8), :] = jnp.zeros((8, K), F32)
    pl.semaphore_wait(barrier, 10)

    def small(j, a, c):
        src, dst = ((own_rows, rows), (own_lists, lists))[j]
        return remote(src, dst.at[me], small_send.at[j, a, c], small_recv.at[j, me], base + c, 2 * core + a)

    def elsewhere(a, c):
        return jnp.logical_not(jnp.logical_and(primary, jnp.logical_and(2 * core + a == me, core == c)))

    for a in range(2):
        for c in range(CORES):
            @pl.when(elsewhere(a, c))
            def _():
                for j in range(2):
                    small(j, a, c).start()

    def piece(o, k):
        return pool.at[o, pl.ds(k * PER, PER)]

    def to_chip(src, o, k, to):
        return remote(src, piece(o, k), send.at[o, k], recv.at[o, k], region, to)

    def to_twin(src, o, k):
        return remote(src, piece(o, k), twin_send.at[o, k], recv.at[o, k], twin, me)

    def own_piece(k):
        return pool_ref.at[pl.ds(k * PER, PER)]

    def relay_out(k):
        return remote(own_piece(DIRECT + k), stop.at[k], r_send.at[0, k], r_recv.at[k], beside, partner)

    def relay_back(k):
        block = piece(partner_beside, DIRECT + k)
        return remote(stop.at[k], block, r_send.at[1, k], recv.at[partner_beside, DIRECT + k], beside, me)

    @pl.when(primary)
    def _():
        def body(k, _):
            @pl.when(k < DIRECT)
            def _():
                to_chip(own_piece(k), me, k, partner).start()

            to_twin(own_piece(k), me, k).start()
            return 0

        lax.fori_loop(0, CHUNKS, body, 0)
        for k in range(RELAYED):
            relay_out(k).start()
        rows[me] = own_rows[...]
        lists[me] = own_lists[...]

    @pl.when(jnp.logical_not(primary))
    def _():
        def body(k, _):
            to_chip(own_piece(k), me, k, cross).start()
            return 0

        lax.fori_loop(0, CHUNKS, body, 0)

    def arrived(o, k):
        to_twin(piece(o, k), o, k).wait_recv()

    def block_grams(o, k):
        for j in range(PER):
            b = k * PER + j
            pert = pool[o, b]
            weight = rows[o, pl.ds(b, 1), :]
            innov = rows[o, pl.ds(POOL + b, 1), :]
            scaled = (pert.astype(F32) * weight).astype(BF)
            lhs = jnp.concatenate([scaled, jnp.broadcast_to(innov, (16, K)).astype(BF)], axis=0)
            res = lax.dot_general(lhs, pert, (((1,), (1,)), ((), ())), preferred_element_type=F32)
            gram[o * SLOTS + b] = res[:K]
            proj[o, pl.ds(b, 1), :] = res[K:K + 1]

    def hand_on(k):
        first = isinstance(k, int)
        if not first or 1 <= k <= RELAYED:
            @pl.when(jnp.logical_and(relay, jnp.logical_and(k >= 1, k <= RELAYED)))
            def _():
                relay_out(k - 1).wait_recv()
                relay_back(k - 1).start()

        @pl.when(k < CHUNKS)
        def _():
            arrived(cross, k)

            @pl.when(primary)
            def _():
                to_chip(piece(cross, k), cross, k, partner).start()
                to_twin(piece(cross, k), cross, k).start()

            arrived(partner, k)

            @pl.when(primary)
            def _():
                to_twin(piece(partner, k), partner, k).start()

        if first:
            return

        @pl.when(k >= 2)
        def _():
            arrived(far, k - 2)

            @pl.when(primary)
            def _():
                to_twin(piece(far, k - 2), far, k - 2).start()

    hand_on(0)
    hand_on(1)
    for o in range(OBS):
        @pl.when(jnp.logical_not(jnp.logical_and(primary, me == o)))
        def _():
            for j, (src, dst) in enumerate(((own_rows, rows), (own_lists, lists))):
                remote(src, dst.at[o], small_send.at[j, 0, 0], small_recv.at[j, o], twin, me).wait_recv()
    to_index = pltpu.make_async_copy(lists, index, in_sem.at[0])
    to_index.start()

    @pl.when(primary)
    def _():
        pltpu.make_async_copy(pool_ref, pool.at[me], local_sem).wait()

    def grams(k):
        @pl.when(jnp.logical_not(primary))
        def _():
            arrived(me, k - 2)

        for o in (me, cross, partner):
            block_grams(o, k - 2)

        @pl.when(k >= 3)
        def _():
            block_grams(far, k - 3)

    def step(k, _):
        hand_on(k)
        grams(k)
        return 0

    def last_step(k, _):
        grams(k)
        hand_on(k)
        return 0

    lax.fori_loop(2, CHUNKS, step, 0)
    lax.fori_loop(CHUNKS, CHUNKS + 2, last_step, 0)
    block_grams(far, CHUNKS - 1)
    to_index.wait()

    def slot(of, g, unit, size):
        return out_ref.at[pl.ds(of * (OWN // UNIT) + g * UNITS + unit, size)]

    def unit_of(g, unit, size):
        return mine.at[pl.ds(g * UNITS + unit, size)]

    def t_first(j, of, g, unit, to):
        return remote(
            unit_of(g, unit, 1), slot(of, g, unit, 1), t_send.at[j, g, unit], t_recv.at[of, g, unit], base + tile, to
        )

    def t_keep(g):
        return pltpu.make_async_copy(unit_of(g, 0, UNITS), slot(solver, g, 0, UNITS), t_local.at[g])

    primary_int = primary.astype(jnp.int32)
    heard = primary_int * partner + (1 - primary_int) * cross
    onward = primary_int * cross + (1 - primary_int) * partner
    part = 1 - primary_int

    def t_pass(of, h, g, c, to):
        half = slot(of, g, h, 1)
        return remote(half, half, f_send.at[c, g], f_recv.at[of, h, g], region, to)

    def forward(g):
        for c in range(CORES):
            of = lax.rem(heard, 2) * CORES + c
            t_first(0, of, g, part, heard).wait_recv()
            t_pass(of, part, g, c, onward).start()

    upper = place_column >= place_row

    def solve_group(g, _):
        matrices, norms, vectors = [], [], []
        for i in range(GROUP):
            c = solver * OWN + g * GROUP + i
            total, vector = None, None
            for o in range(OBS):
                for m in range(2):
                    b = index[o, m, c]
                    one, row = gram[o * SLOTS + b], proj[o, pl.ds(b, 1), :]
                    total = one if total is None else total + one
                    vector = row if vector is None else vector + row
            matrix = eye + total * (1.0 / 127.0)
            square = jnp.sum(jnp.sum(matrix * matrix, axis=0, keepdims=True), axis=1, keepdims=True)
            scale = lax.rsqrt(square)
            matrices.append(matrix * scale)
            norms.append(scale)
            vectors.append(vector)
        full = inverse_root(matrices, eye)
        for u in range(UNITS):
            extra = []
            for q in range(UNIT // 2):
                roots, means = [], []
                for i in (u * UNIT + 2 * q, u * UNIT + 2 * q + 1):
                    row = vectors[i] * (norms[i] * (1.0 / 127.0))
                    column = jnp.sum(full[i] * row, axis=1, keepdims=True)
                    row = jnp.sum(full[i] * column, axis=0, keepdims=True)
                    roots.append(full[i] * jnp.sqrt(norms[i]))
                    means += split(row)
                extra += [jnp.sum(roots[1] * eye, axis=0, keepdims=True).astype(BF)] + means
                mine[g * UNITS + u, pl.ds(q * K, K), :] = jnp.where(upper, roots[0], roots[1]).astype(BF)
            extra.append(jnp.zeros((16 - len(extra), K), BF))
            mine[g * UNITS + u, pl.ds(UNIT // 2 * K, 16), :] = jnp.concatenate(extra, axis=0)
        for j, unit, to in ((0, 0, partner), (1, 1, cross), (0, 1, partner), (1, 0, cross)):
            t_first(j, solver, g, unit, to).start()

        @pl.when(primary)
        def _():
            t_keep(g).start()

        @pl.when(jnp.logical_not(primary))
        def _():
            for unit in range(UNITS):
                t_first(2, solver, g, unit, me).start()

        @pl.when(g > 0)
        def _():
            forward(g - 1)

        return 0

    lax.fori_loop(0, GROUPS, solve_group, 0)
    forward(GROUPS - 1)

    @pl.when(primary)
    def _():
        for g in range(GROUPS):
            for unit in range(UNITS):
                t_first(2, lax.rem(me, 2) * CORES + 1 - core, g, unit, me).wait_recv()
            t_keep(g).wait()

        for k in range(DIRECT):
            to_chip(own_piece(k), me, k, partner).wait_send()
        for k in range(RELAYED):
            relay_out(k).wait_send()
        for k in range(CHUNKS):
            to_chip(piece(cross, k), cross, k, partner).wait_send()
            to_twin(own_piece(k), me, k).wait_send()
            for o in (cross, partner, far):
                to_twin(piece(o, k), o, k).wait_send()

    @pl.when(jnp.logical_not(primary))
    def _():
        for g in range(GROUPS):
            for c in range(CORES):
                of = lax.rem(far, 2) * CORES + c
                for h in range(2):
                    t_pass(of, h, g, c, onward).wait_recv()
            for unit in range(UNITS):
                t_first(2, solver, g, unit, me).wait_send()

        for k in range(CHUNKS):
            to_chip(own_piece(k), me, k, cross).wait_send()

    for g in range(GROUPS):
        for unit in range(UNITS):
            t_first(0, solver, g, unit, partner).wait_send()
            t_first(1, solver, g, unit, cross).wait_send()
        for c in range(CORES):
            of = lax.rem(heard, 2) * CORES + c
            t_first(0, of, g, 1 - part, heard).wait_recv()
            t_pass(of, part, g, c, onward).wait_send()
    @pl.when(relay)
    def _():
        for k in range(RELAYED):
            relay_back(k).wait_send()

    for a in range(2):
        for c in range(CORES):
            @pl.when(elsewhere(a, c))
            def _():
                for j in range(2):
                    small(j, a, c).wait_send()


APPLY = 32


def apply_kernel(clusters, count_ref, packed_ref, x_ref, mean_ref, out_ref, counts, packed_in, x_in, mean, result, in_sem, out_sem):
    steps = clusters // APPLY

    def reads(s):
        here, units = pl.ds(s * APPLY, APPLY), pl.ds(s * (APPLY // UNIT), APPLY // UNIT)
        return (
            pltpu.make_async_copy(packed_ref.at[units], packed_in.at[units], in_sem.at[0, s]),
            pltpu.make_async_copy(x_ref.at[here], x_in.at[here], in_sem.at[1, s]),
        )

    def write(s):
        here = pl.ds(s * APPLY, APPLY)
        return pltpu.make_async_copy(result.at[here], out_ref.at[here], out_sem.at[s])

    small = (
        pltpu.make_async_copy(count_ref, counts, in_sem.at[0, steps]),
        pltpu.make_async_copy(mean_ref, mean, in_sem.at[1, steps]),
    )
    for c in reads(0) + small:
        c.start()
    for s in range(1, steps):
        for c in reads(s):
            c.start()
    place_row, place_column = places()
    diagonal, upper, lower = place_row == place_column, place_column >= place_row, place_column < place_row

    eye = diagonal.astype(BF)
    for c in small:
        c.wait()
    count = counts[lax.axis_index("region")]

    def body(s, _):
        for c in reads(s):
            c.wait()
        for u in range(APPLY // UNIT):
            unit = s * (APPLY // UNIT) + u
            extra = packed_in[unit, pl.ds(UNIT // 2 * K, 16), :].astype(F32)
            for q in range(UNIT // 2):
                packed = packed_in[unit, pl.ds(q * K, K), :]
                straight = packed.astype(F32)
                turned = straight.T
                roots = (
                    jnp.where(upper, straight, turned),
                    jnp.where(lower, straight, jnp.where(diagonal, extra[5 * q:5 * q + 1], turned)),
                )
                for i in range(2):
                    c = unit * UNIT + 2 * q + i
                    m = 5 * q + 1 + 2 * i
                    solved = (roots[i] + (extra[m:m + 1] + extra[m + 1:m + 2])).astype(BF)
                    solved = jnp.where(c < count, solved, eye)
                    mixed = jnp.dot(solved, x_in[c], preferred_element_type=F32)
                    result[c] = (mixed + mean[pl.ds(c, 1), :]).astype(BF)
        write(s).start()
        return 0

    lax.fori_loop(0, steps, body, 0)
    for s in range(steps):
        write(s).wait()


def local(
    state_pert, state_mean, obs_pert, innov, obs_weight, block_type, type_prec, block_list, block_count, obs_clusters
):
    clusters, members, points = state_pert.shape
    dma = pltpu.SemaphoreType.DMA
    hbm, anywhere = pl.BlockSpec(memory_space=pltpu.HBM), pl.BlockSpec(memory_space=pl.ANY)
    packed = pl.pallas_call(
        solve_kernel,
        out_shape=jax.ShapeDtypeStruct((clusters // UNIT, PACKED, members), BF),
        in_specs=[hbm] * 7,
        out_specs=anywhere,
        scratch_shapes=[
            pltpu.VMEM((2, clusters), jnp.int32),
            pltpu.VMEM((1, clusters), jnp.int32),
            pltpu.SMEM((POOL,), jnp.int32),
            pltpu.SMEM(type_prec.shape, F32),
            pltpu.VMEM((POOL, K), F32),
            pltpu.VMEM((POOL, K), F32),
            pltpu.VMEM((OBS, POOL, members, K), BF),
            pltpu.VMEM((2 * POOL, K), F32),
            pltpu.VMEM((8, clusters), jnp.int32),
            pltpu.VMEM((OBS, 2 * POOL, K), F32),
            pltpu.VMEM((OBS, 8, clusters), jnp.int32),
            pltpu.SMEM((OBS, 8, clusters), jnp.int32),
            pltpu.VMEM((OBS * SLOTS, members, members), F32),
            pltpu.VMEM((OBS, POOL + 8, members), F32),
            pltpu.VMEM((OWN // UNIT, PACKED, members), BF),
            pltpu.VMEM((RELAYED, PER, members, K), BF),
            dma((6,)), dma,
            dma((2, 2, CORES)), dma((2, OBS)),
            dma((OBS, CHUNKS)), dma((OBS, CHUNKS)), dma((OBS, CHUNKS)),
            dma((2, RELAYED)), dma((RELAYED,)),
            dma((GROUPS,)),
            dma((3, GROUPS, UNITS)), dma((OBS, GROUPS, UNITS)),
            dma((CORES, GROUPS)), dma((OBS, 2, GROUPS)),
        ],
        compiler_params=pltpu.CompilerParams(
            collective_id=0, has_side_effects=True, vmem_limit_bytes=60 << 20
        ),
        name="solve",
    )(block_list.T, block_count.T, block_type, type_prec, obs_weight, innov, obs_pert)
    return pl.pallas_call(
        functools.partial(apply_kernel, clusters),
        out_shape=jax.ShapeDtypeStruct(state_pert.shape, BF),
        in_specs=[hbm] * 4,
        out_specs=hbm,
        scratch_shapes=[
            pltpu.SMEM(obs_clusters.shape, jnp.int32),
            pltpu.VMEM(packed.shape, BF), pltpu.VMEM(state_pert.shape, BF),
            pltpu.VMEM(state_mean.shape, F32), pltpu.VMEM(state_pert.shape, BF),
            dma((2, clusters // APPLY + 1)), dma((clusters // APPLY,)),
        ],
        compiler_params=pltpu.CompilerParams(vmem_limit_bytes=58 << 20),
        name="apply",
    )(obs_clusters, packed, state_pert, state_mean)


def solution(mesh):
    placed = (
        P("region", None, "obs"),
        P("region", "obs"),
        P(("region", "obs"), None, None),
        P(("region", "obs"), None),
        P(("region", "obs"), None),
        P(("region", "obs")),
        P(),
        P("region", "obs"),
        P("region", "obs"),
        P(),
    )
    return jax.shard_map(
        local, mesh=mesh, in_specs=placed, out_specs=P("region", None, "obs"), check_vma=False
    )
```
